256 devices in a mesh: tile: 64 (over y, z_lo, x), head: 4 (over z_hi, core).
Axes of the slice: x: 4, y: 4, z: 8 (z_hi: 2, z_lo: 4; z = z_hi * 4 + z_lo), core: 2. Of those that a mesh axis runs over, the one named last changes fastest.
Arguments:
- tokens: bfloat16 [16384, 384], P('tile'), may hold values from -6 to 6
- ln_gain: float32 [384], replicated, may hold values from 0.1 to 1.9
- qkv_weight: bfloat16 [3, 768, 384], P(None, 'head'), may hold values from -0.3125 to 0.3125
- query_pool: bfloat16 [4, 768], P(None, 'head'), may hold values from -3 to 3
- key_pool: bfloat16 [16, 768], P(None, 'head'), may hold values from -1.5 to 1.5
- value_pool: bfloat16 [16, 768], P(None, 'head'), may hold values from -1.5 to 1.5
- proj_weight: bfloat16 [768, 768], P('head'), may hold values from -0.21875 to 0.21875
- skip_weight: bfloat16 [768, 384], P('head'), may hold values from -0.3125 to 0.3125
- cotangent: bfloat16 [4096, 768], P('tile', 'head'), may hold values from -6 to 6
Outputs:
- block_out: bfloat16 [4096, 768], P('tile', 'head')
- input_grad: bfloat16 [16384, 384], P('tile')
- qkv_grad: float32 [3, 768, 384], P(None, 'head')
- proj_grad: float32 [768, 768], P('head')
The draws below stay inside these ranges and needn't reach their ends.
All inputs are finite; a program needn't handle non-finite values.
Results may differ from the reference program's by a relative error of at most 0.02.
Values may be sent and summed in bfloat16 or wider, within the bound.
No kernel may reach another device: no remote copies, remote signals or barrier semaphores. Data moves between devices by JAX's collectives and lax.ppermute only.
A program may use at most 64 MiB of HBM per device.

```python
import jax
import jax.numpy as jnp
from jax import lax

C_IN = 384
C_OUT = 768
HEADS = 8
HEAD_DIM = 96
TILE_H = 8
TILE_W = 32
TOKENS = 16384
N_TILE = 64


def shard_levels(stream_key, extent, pieces, low, top_value):
    def one(dim, parts):
        heights = jax.random.uniform(jax.random.fold_in(jax.random.fold_in(stream_key, 6), dim), (parts,), jnp.float32, low / len(pieces), top_value / len(pieces))
        return jnp.repeat(jnp.exp(heights), extent[dim] // parts).reshape((-1,) + (1,) * (len(extent) - dim - 1))

    loudness = one(*pieces[0])
    for cut in pieces[1:]:
        loudness = loudness * one(*cut)
    return loudness


def noise(key, extent, scale, limit, shards=(), held_as=jnp.bfloat16):
    entries = jax.random.normal(key, extent, jnp.float32) * scale
    if len(shards) > 0:
        entries = shard_levels(key, extent, shards, -0.22, 0.18) * entries
    return jnp.clip(entries, min=-limit, max=limit).astype(held_as)


def setup_inputs(seed: int = 0) -> dict:
    streams_of = jax.random.split(jax.random.key(seed), 10)
    return {
        "tokens": noise(streams_of[0], (TOKENS, C_IN), 1.0, 6.0, ((0, 64),)),
        "ln_gain": jnp.clip(1.0 + 0.18 * jax.random.normal(streams_of[1], (C_IN,), jnp.float32), 0.1, 1.9),
        "qkv_weight": noise(streams_of[2], (3, C_OUT, C_IN), C_IN ** -0.5, 0.3125, ((1, 4),)),
        "query_pool": noise(streams_of[3], (4, C_OUT), 4 ** -0.5, 3.0, ((1, 4),)),
        "key_pool": noise(streams_of[4], (16, C_OUT), 16 ** -0.5, 1.5, ((1, 4),)),
        "value_pool": noise(streams_of[5], (16, C_OUT), 16 ** -0.5, 1.5, ((1, 4),)),
        "proj_weight": noise(streams_of[6], (C_OUT, C_OUT), C_OUT ** -0.5, 0.21875, ((0, 4),)),
        "skip_weight": noise(streams_of[7], (C_OUT, C_IN), C_IN ** -0.5, 0.3125, ((0, 4),)),
        "cotangent": noise(streams_of[8], (TOKENS // 4, C_OUT), 1.0, 6.0, ((0, 64), (1, 4))),
    }


EPSILON = 1e-06

def normalize(tokens):
    values_in = tokens.astype(jnp.float32)
    center = values_in - lax.optimization_barrier(jnp.mean(values_in, axis=-1, keepdims=True))
    inv_std = lax.rsqrt(lax.optimization_barrier(jnp.mean(center * center, axis=-1, keepdims=True)) + EPSILON)
    return (center * inv_std, inv_std)

def pool_field(feature, weight, stride):
    channels = feature.shape[-1]
    cells_grid = feature.reshape(-1, TILE_H // stride, stride, TILE_W // stride, stride, channels)
    kernel = weight.astype(jnp.float32).reshape(stride, stride, channels)
    return jnp.einsum('fiajbc,abc->fijc', cells_grid, kernel).reshape(-1, channels)

def spread_field(upstream, weight, stride):
    channels = upstream.shape[-1]
    cells_grid = upstream.reshape(-1, TILE_H // stride, TILE_W // stride, channels)
    kernel = weight.astype(jnp.float32).reshape(stride, stride, channels)
    return jnp.einsum('fijc,abc->fiajbc', cells_grid, kernel).reshape(-1, channels)

def mean_pool(tokens):
    channels = tokens.shape[-1]
    cells_grid = tokens.astype(jnp.float32).reshape(-1, TILE_H // 2, 2, TILE_W // 2, 2, channels)
    return lax.optimization_barrier(jnp.sum(cells_grid, axis=(2, 4))).reshape(-1, channels) * 0.25

def expand_rows(upstream):
    channels = upstream.shape[-1]
    cells_grid = upstream.reshape(-1, TILE_H // 2, 1, TILE_W // 2, 1, channels)
    cells_grid = jnp.broadcast_to(cells_grid, (cells_grid.shape[0], TILE_H // 2, 2, TILE_W // 2, 2, channels))
    return cells_grid.reshape(-1, channels)

def norm_back(upstream, unit_rows, inv_std, ln_gain):
    scaled = upstream * ln_gain
    return inv_std * (scaled - lax.optimization_barrier(jnp.mean(scaled, axis=-1, keepdims=True)) - unit_rows * lax.optimization_barrier(jnp.mean(scaled * unit_rows, axis=-1, keepdims=True)))

def attend(queries, grad_rows, key_rows, value_rows):
    scale = HEAD_DIM ** (-0.5)
    scores = jnp.dot(queries, key_rows.T, preferred_element_type=jnp.float32) * scale
    exp_scores = jnp.exp(scores)
    row_total = lax.optimization_barrier(jnp.sum(exp_scores, axis=-1, keepdims=True))
    attn_probs = (exp_scores / row_total).astype(jnp.bfloat16)
    out_rows = (jnp.dot(attn_probs, value_rows, preferred_element_type=jnp.float32) + queries.astype(jnp.float32)).astype(jnp.bfloat16)
    dprobs = jnp.dot(grad_rows, value_rows.T, preferred_element_type=jnp.float32)
    probs_wide = attn_probs.astype(jnp.float32)
    row_delta = lax.optimization_barrier(jnp.sum(probs_wide * dprobs, axis=-1, keepdims=True))
    d_scores = (scale * probs_wide * (dprobs - row_delta)).astype(jnp.bfloat16)
    dquery = jnp.dot(d_scores, key_rows, preferred_element_type=jnp.float32) + grad_rows.astype(jnp.float32)
    key_grad = jnp.dot(d_scores.T, queries, preferred_element_type=jnp.float32)
    value_grad = jnp.dot(attn_probs.T, grad_rows, preferred_element_type=jnp.float32)
    return (out_rows, dquery, key_grad, value_grad, row_total[:, 0], row_delta[:, 0])

def head_pass(operands):
    queries, grad_rows, key_rows, value_rows = operands

    def scan_step(accum, query_block):
        out_rows, dquery, key_grad, value_grad, row_total, row_delta = attend(query_block[0], query_block[1], key_rows, value_rows)
        return ((accum[0] + key_grad, accum[1] + value_grad), (out_rows, dquery))
    zero_grad = jnp.zeros(key_rows.shape, jnp.float32)
    accum, results = lax.scan(scan_step, (zero_grad, zero_grad), (queries, grad_rows))
    return (results[0], results[1], accum[0], accum[1])

def split_heads(rows_in, blocks):
    return rows_in.reshape(rows_in.shape[0], HEADS, HEAD_DIM).transpose(1, 0, 2).reshape(HEADS, blocks, -1, HEAD_DIM)

def join_heads(stacked):
    return stacked.reshape(HEADS, -1, HEAD_DIM).transpose(1, 0, 2).reshape(-1, C_OUT)

def reference(tokens, ln_gain, qkv_weight, query_pool, key_pool, value_pool, proj_weight, skip_weight, cotangent):
    unit_rows, inv_std = normalize(tokens)
    normed = (unit_rows * ln_gain).astype(jnp.bfloat16)
    projected = [jnp.dot(normed, qkv_weight[which].T, preferred_element_type=jnp.float32) for which in range(3)]
    query_pooled = pool_field(projected[0], query_pool, 2).astype(jnp.bfloat16)
    key_pooled = pool_field(projected[1], key_pool, 4).astype(jnp.bfloat16)
    value_pooled = pool_field(projected[2], value_pool, 4).astype(jnp.bfloat16)
    d_attended = jnp.dot(cotangent, proj_weight.T, preferred_element_type=jnp.float32).astype(jnp.bfloat16)
    head_outs, query_grads, key_grads, value_grads = lax.map(head_pass, (split_heads(query_pooled, N_TILE), split_heads(d_attended, N_TILE), split_heads(key_pooled, 1)[:, 0], split_heads(value_pooled, 1)[:, 0]))
    attended = join_heads(head_outs)
    pooled_input = mean_pool(tokens).astype(jnp.bfloat16)
    block_out = (jnp.dot(attended, proj_weight, preferred_element_type=jnp.float32) + jnp.dot(pooled_input, skip_weight.T, preferred_element_type=jnp.float32)).astype(jnp.bfloat16)
    proj_grad = jnp.dot(attended.T, cotangent, preferred_element_type=jnp.float32)
    d_pooled = jnp.dot(cotangent, skip_weight, preferred_element_type=jnp.float32)
    d_projected = jnp.stack([spread_field(join_heads(query_grads), query_pool, 2), spread_field(join_heads(key_grads), key_pool, 4), spread_field(join_heads(value_grads), value_pool, 4)]).astype(jnp.bfloat16)
    qkv_grad = jnp.stack([jnp.dot(d_projected[which].T, normed, preferred_element_type=jnp.float32) for which in range(3)])
    d_normed = jnp.dot(d_projected[0], qkv_weight[0], preferred_element_type=jnp.float32)
    d_normed = d_normed + jnp.dot(d_projected[1], qkv_weight[1], preferred_element_type=jnp.float32)
    d_normed = d_normed + jnp.dot(d_projected[2], qkv_weight[2], preferred_element_type=jnp.float32)
    input_grad = (norm_back(d_normed, unit_rows, inv_std, ln_gain) + expand_rows(d_pooled) * 0.25).astype(jnp.bfloat16)
    return (block_out, input_grad, qkv_grad, proj_grad)
```

```python
import jax
import jax.numpy as jnp
from jax import lax
from jax.sharding import PartitionSpec as P

HEAD_DIM = 96
TILE_H = 8
TILE_W = 32
EPSILON = 1e-06
F32 = jnp.float32
BF16 = jnp.bfloat16
STRIDES = {"y": 16, "z": 4, "x": 1}


def shift(block, axis, step):
    stride = STRIDES[axis]
    pairs = []
    for index in range(64):
        place = (index // stride) % 4
        pairs.append((index, index + ((place + step) % 4 - place) * stride))
    return lax.ppermute(block, "tile", pairs)


def swap_core(block):
    return lax.ppermute(block, "head", [(i, i ^ 1) for i in range(4)])


def swap_half(block):
    return lax.ppermute(block, "head", [(i, i ^ 2) for i in range(4)])


def gather_axis(block, axis):
    return jnp.stack([block] + [shift(block, axis, k) for k in (1, 2, 3)])


def sum_four(parts):
    wide = [p.astype(F32) for p in parts]
    return (wide[0] + wide[2]) + (wide[1] + wide[3])


def scatter_axis(blocks, axis):
    return sum_four([blocks[0]] + [shift(blocks[k], axis, -k) for k in (1, 2, 3)])


def sum_axis(block, axis):
    return sum_four([block] + [shift(block, axis, k) for k in (1, 2, 3)])


def all_sum(part, place_x):
    rows, columns = part.shape
    chunks = part.astype(BF16).reshape(4, rows // 4, columns)
    rolled = jnp.concatenate([chunks, chunks])
    ahead = [
        lax.dynamic_index_in_dim(rolled, place_x + k, 0, keepdims=False) for k in range(4)
    ]
    own = sum_four([ahead[0]] + [shift(ahead[k], "x", k) for k in (1, 2, 3)])
    own = sum_axis(own.astype(BF16), "y")
    own = sum_axis(own.astype(BF16), "z").astype(BF16)
    back = [own] + [shift(own, "x", k) for k in (1, 2, 3)]
    ordered = jnp.stack([back[0], back[3], back[2], back[1]])
    doubled = jnp.concatenate([ordered, ordered])
    placed = lax.dynamic_slice_in_dim(doubled, (4 - place_x) % 4, 4, 0)
    return placed.reshape(rows, columns).astype(F32)


def normalize(tokens):
    values_in = tokens.astype(F32)
    center = values_in - jnp.mean(values_in, axis=-1, keepdims=True)
    inv_std = lax.rsqrt(jnp.mean(center * center, axis=-1, keepdims=True) + EPSILON)
    return (center * inv_std, inv_std)


def pool_field(feature, weight, stride):
    channels = feature.shape[-1]
    cells_grid = feature.reshape(-1, TILE_H // stride, stride, TILE_W // stride, stride, channels)
    kernel = weight.astype(F32).reshape(stride, stride, channels)
    return jnp.einsum("fiajbc,abc->fijc", cells_grid, kernel).reshape(-1, channels)


def spread_field(upstream, weight, stride):
    channels = upstream.shape[-1]
    cells_grid = upstream.reshape(-1, TILE_H // stride, TILE_W // stride, channels)
    kernel = weight.astype(F32).reshape(stride, stride, channels)
    return jnp.einsum("fijc,abc->fiajbc", cells_grid, kernel).reshape(-1, channels)


def mean_pool(tokens):
    channels = tokens.shape[-1]
    cells_grid = tokens.astype(F32).reshape(-1, TILE_H // 2, 2, TILE_W // 2, 2, channels)
    return jnp.sum(cells_grid, axis=(2, 4)).reshape(-1, channels) * 0.25


def expand_rows(upstream):
    channels = upstream.shape[-1]
    cells_grid = upstream.reshape(-1, TILE_H // 2, 1, TILE_W // 2, 1, channels)
    cells_grid = jnp.broadcast_to(
        cells_grid, (cells_grid.shape[0], TILE_H // 2, 2, TILE_W // 2, 2, channels)
    )
    return cells_grid.reshape(-1, channels)


def norm_back(upstream, unit_rows, inv_std, ln_gain):
    scaled = upstream * ln_gain
    return inv_std * (
        scaled
        - jnp.mean(scaled, axis=-1, keepdims=True)
        - unit_rows * jnp.mean(scaled * unit_rows, axis=-1, keepdims=True)
    )


def attend(queries, grad_rows, key_rows, value_rows):
    scale = HEAD_DIM ** (-0.5)
    scores = jnp.dot(queries, key_rows.T, preferred_element_type=F32) * scale
    exp_scores = jnp.exp(scores)
    row_total = jnp.sum(exp_scores, axis=-1, keepdims=True)
    attn_probs = (exp_scores / row_total).astype(BF16)
    out_rows = (
        jnp.dot(attn_probs, value_rows, preferred_element_type=F32) + queries.astype(F32)
    ).astype(BF16)
    dprobs = jnp.dot(grad_rows, value_rows.T, preferred_element_type=F32)
    probs_wide = attn_probs.astype(F32)
    row_delta = jnp.sum(probs_wide * dprobs, axis=-1, keepdims=True)
    d_scores = (scale * probs_wide * (dprobs - row_delta)).astype(BF16)
    dquery = jnp.dot(d_scores, key_rows, preferred_element_type=F32) + grad_rows.astype(F32)
    key_grad = jnp.dot(d_scores.T, queries, preferred_element_type=F32)
    value_grad = jnp.dot(attn_probs.T, grad_rows, preferred_element_type=F32)
    return (out_rows, dquery, key_grad, value_grad)


def heads_of(rows_in):
    return [rows_in[:, :HEAD_DIM], rows_in[:, HEAD_DIM:]]


def local(
    tokens,
    ln_gain,
    qkv_weight,
    query_pool,
    key_pool,
    value_pool,
    proj_weight,
    skip_weight,
    cotangent,
):
    place_x = lax.axis_index("tile") % 4
    head = lax.axis_index("head")
    core, half = head % 2, head // 2
    unit_rows, inv_std = normalize(tokens)
    normed = (unit_rows * ln_gain).astype(BF16)

    def project(which):
        return jnp.dot(normed, qkv_weight[which].T, preferred_element_type=F32)

    key_pooled = pool_field(project(1), key_pool, 4).astype(BF16)
    value_pooled = pool_field(project(2), value_pool, 4).astype(BF16)
    gathered = jnp.stack([key_pooled, value_pooled])
    for axis in ("z", "y", "x"):
        gathered = gather_axis(gathered, axis)
    all_keys = gathered[:, :, :, 0].reshape(1024, -1)
    all_values = gathered[:, :, :, 1].reshape(1024, -1)

    other = swap_core(cotangent)
    pair = jnp.where(
        core == 0,
        jnp.concatenate([cotangent, other], axis=1),
        jnp.concatenate([other, cotangent], axis=1),
    )
    far = swap_half(pair)
    full_cotangent = jnp.where(
        half == 0, jnp.concatenate([pair, far], axis=1), jnp.concatenate([far, pair], axis=1)
    )
    d_pooled_part = jnp.dot(cotangent, skip_weight, preferred_element_type=F32).astype(BF16)
    d_pooled = (d_pooled_part.astype(F32) + swap_core(d_pooled_part).astype(F32)).astype(BF16)
    d_pooled = d_pooled.astype(F32) + swap_half(d_pooled).astype(F32)

    query_pooled = pool_field(project(0), query_pool, 2).astype(BF16)
    d_attended = jnp.dot(full_cotangent, proj_weight.T, preferred_element_type=F32).astype(BF16)

    results = [
        attend(*operands)
        for operands in zip(
            heads_of(query_pooled), heads_of(d_attended), heads_of(all_keys), heads_of(all_values)
        )
    ]
    attended, query_grad, key_grads, value_grads = [
        jnp.concatenate([results[0][i], results[1][i]], axis=1) for i in range(4)
    ]

    grads = jnp.stack(
        [key_grads.reshape(4, 4, 4, 16, -1), value_grads.reshape(4, 4, 4, 16, -1)], axis=3
    ).astype(BF16)
    for axis in ("x", "y", "z"):
        grads = scatter_axis(grads.astype(BF16), axis)

    d_queries = spread_field(query_grad, query_pool, 2).astype(BF16)
    first_part = jnp.concatenate(
        [
            jnp.dot(d_queries.T, normed, preferred_element_type=F32),
            jnp.dot(attended.T, full_cotangent, preferred_element_type=F32),
        ],
        axis=1,
    )
    first_sum = all_sum(first_part, place_x)

    head_part = jnp.dot(attended, proj_weight, preferred_element_type=F32).astype(BF16)
    quarters = head_part.reshape(64, 2, 2, 192)
    mine = lax.dynamic_index_in_dim(quarters, core, 2, keepdims=False)
    theirs = lax.dynamic_index_in_dim(quarters, 1 - core, 2, keepdims=False)
    both = (mine.astype(F32) + swap_core(theirs).astype(F32)).astype(BF16)
    kept = lax.dynamic_index_in_dim(both, half, 1, keepdims=False)
    sent = lax.dynamic_index_in_dim(both, 1 - half, 1, keepdims=False)
    summed = kept.astype(F32) + swap_half(sent).astype(F32)
    pooled_input = mean_pool(tokens).astype(BF16)
    block_out = (
        summed + jnp.dot(pooled_input, skip_weight.T, preferred_element_type=F32)
    ).astype(BF16)

    d_keys = spread_field(grads[0], key_pool, 4).astype(BF16)
    d_values = spread_field(grads[1], value_pool, 4).astype(BF16)
    second_part = jnp.concatenate(
        [
            jnp.dot(d_keys.T, normed, preferred_element_type=F32),
            jnp.dot(d_values.T, normed, preferred_element_type=F32),
        ],
        axis=1,
    )
    second_sum = all_sum(second_part, place_x)

    d_normed_part = jnp.dot(d_queries, qkv_weight[0], preferred_element_type=F32)
    d_normed_part = d_normed_part + jnp.dot(d_keys, qkv_weight[1], preferred_element_type=F32)
    d_normed_part = d_normed_part + jnp.dot(d_values, qkv_weight[2], preferred_element_type=F32)
    halves = d_normed_part.astype(BF16).reshape(2, 128, -1)

    def own_half(rows_in):
        return lax.dynamic_slice_in_dim(rows_in, core * 128, 128, 0)

    kept_rows = lax.dynamic_index_in_dim(halves, core, 0, keepdims=False)
    sent_rows = lax.dynamic_index_in_dim(halves, 1 - core, 0, keepdims=False)
    row_sum = (kept_rows.astype(F32) + swap_core(sent_rows).astype(F32)).astype(BF16)
    d_normed = row_sum.astype(F32) + swap_half(row_sum).astype(F32)
    own_rows = (
        norm_back(d_normed, own_half(unit_rows), own_half(inv_std), ln_gain)
        + own_half(expand_rows(d_pooled)) * 0.25
    ).astype(BF16)
    other_rows = swap_core(own_rows)
    input_grad = jnp.where(
        core == 0,
        jnp.concatenate([own_rows, other_rows]),
        jnp.concatenate([other_rows, own_rows]),
    )
    qkv_grad = jnp.stack([first_sum[:, :384], second_sum[:, :384], second_sum[:, 384:]])
    return (block_out, input_grad, qkv_grad, first_sum[:, 384:])


def solution(mesh):
    placed = (
        P("tile", None),
        P(),
        P(None, "head", None),
        P(None, "head"),
        P(None, "head"),
        P(None, "head"),
        P("head", None),
        P("head", None),
        P("tile", "head"),
    )
    return jax.shard_map(
        local,
        mesh=mesh,
        in_specs=placed,
        out_specs=(P("tile", "head"), P("tile", None), P(None, "head", None), P("head", None)),
        check_vma=False,
    )
```

```python
import numpy as np

import jax
import jax.numpy as jnp
from jax import lax
from jax.experimental import pallas as pl
from jax.experimental.pallas import tpu as pltpu
from jax.sharding import Mesh
from jax.sharding import PartitionSpec as P

HEAD_DIM = 96
EPSILON = 1e-06
F32 = jnp.float32
BF16 = jnp.bfloat16
TILE = ("y", "z", "x")
HEAD = ("half", "core")
PLANE = ("y", "x")


def shift(block, axis, step):
    return lax.ppermute(block, axis, [(i, (i + step) % 4) for i in range(4)])


def swap(block, axis):
    return lax.ppermute(block, axis, [(0, 1), (1, 0)])


def exchange_plane(blocks):
    return lax.all_to_all(blocks, PLANE, 0, 0, tiled=True)


def gather_plane(block):
    return exchange_plane(jnp.broadcast_to(block[None], (16, *block.shape)))


def sum_four(parts):
    wide = [p.astype(F32) for p in parts]
    return (wide[0] + wide[2]) + (wide[1] + wide[3])


def fuse(function, outs, name):
    def call(*operands):
        count = len(operands)

        def kernel(*refs):
            results = function(*[ref[...] for ref in refs[:count]])
            for ref, result in zip(refs[count:], results):
                ref[...] = result

        return pl.pallas_call(
            kernel,
            out_shape=[jax.ShapeDtypeStruct(shape, dtype) for shape, dtype in outs],
            compiler_params=pltpu.CompilerParams(vmem_limit_bytes=48 * 1024 * 1024),
            name=name,
        )(*operands)

    return call


def dot(a, b, contract):
    return lax.dot_general(a, b, (contract, ((), ())), preferred_element_type=F32)


def dot_nn(a, b):
    return dot(a, b, ((1,), (0,)))


def dot_nt(a, b):
    return dot(a, b, ((1,), (1,)))


def dot_tn(a, b):
    return dot(a, b, ((0,), (0,)))


def token_of(place):
    a, b, r, c = place >> 6, (place >> 4) & 3, (place >> 3) & 1, place & 7
    return (4 * r + a) * 32 + 4 * c + b


def query_of(place):
    a, b, r, c = place >> 5, (place >> 4) & 1, (place >> 3) & 1, place & 7
    return (2 * r + a) * 16 + 2 * c + b


def selector(count, source, transposed):
    rows = lax.broadcasted_iota(jnp.int32, (count, count), 0)
    columns = lax.broadcasted_iota(jnp.int32, (count, count), 1)
    hit = source(columns) == rows if transposed else source(rows) == columns
    return jnp.where(hit, 1.0, 0.0).astype(BF16)


def normalize(values_in):
    center = values_in - jnp.mean(values_in, axis=-1, keepdims=True)
    inv_std = lax.rsqrt(jnp.mean(center * center, axis=-1, keepdims=True) + EPSILON)
    return center * inv_std, inv_std


def pool_keys(feature, weight):
    wide = weight.astype(F32)
    total = wide[0:1] * feature[0:16]
    for k in range(1, 16):
        total = total + wide[k : k + 1] * feature[16 * k : 16 * k + 16]
    return total


def spread_keys(upstream, weight):
    wide = weight.astype(F32)
    return jnp.concatenate([wide[k : k + 1] * upstream for k in range(16)], axis=0)


def query_blocks():
    out = []
    for a2 in range(2):
        for b2 in range(2):
            out.append(
                [
                    (2 * a1 + b1, (2 * a2 + a1) * 4 + 2 * b2 + b1)
                    for a1 in range(2)
                    for b1 in range(2)
                ]
            )
    return out


def pool_queries(feature, weight):
    wide = weight.astype(F32)
    rows = []
    for members in query_blocks():
        total = None
        for tap, block in members:
            term = feature[16 * block : 16 * block + 16]
            if weight is not None:
                term = wide[tap : tap + 1] * term
            total = term if total is None else total + term
        rows.append(total)
    return jnp.concatenate(rows, axis=0)


def spread_queries(upstream, weight):
    wide = weight.astype(F32)
    blocks = [None] * 16
    for place, members in enumerate(query_blocks()):
        for tap, block in members:
            blocks[block] = wide[tap : tap + 1] * upstream[16 * place : 16 * place + 16]
    return jnp.concatenate(blocks, axis=0)


def front(tokens, ln_gain, weight_kv, key_pool, value_pool):
    held = dot_nn(selector(256, token_of, False), tokens)
    unit, _ = normalize(held)
    normed = (unit * ln_gain).astype(BF16)
    key_pooled = pool_keys(dot_nt(normed, weight_kv[1]), key_pool)
    value_pooled = pool_keys(dot_nt(normed, weight_kv[2]), value_pool)
    both = jnp.concatenate([key_pooled, value_pooled], axis=1).astype(BF16)
    return both, normed, held.astype(BF16)


def middle(normed, held, weight_q, query_pool, full_cotangent, cotangent, proj_weight, skip_weight):
    query_pooled = pool_queries(dot_nt(normed, weight_q[0]), query_pool).astype(BF16)
    to_held = selector(64, query_of, False)
    held_cotangent = dot_nn(to_held, full_cotangent).astype(BF16)
    d_attended = dot_nt(held_cotangent, proj_weight).astype(BF16)
    ones = jnp.ones((4, held.shape[1]), F32)
    pooled_input = (pool_queries(held.astype(F32), ones) * 0.25).astype(BF16)
    natural = dot_nn(selector(64, query_of, True), pooled_input).astype(BF16)
    skipped = dot_nt(natural, skip_weight)
    own_cotangent = dot_nn(to_held, cotangent).astype(BF16)
    d_pooled = dot_nn(own_cotangent, skip_weight).astype(BF16)
    return query_pooled, d_attended, held_cotangent, skipped, d_pooled


def attend(rows_kv, query_pooled, d_attended):
    rows_kv = rows_kv.reshape(1024, 384)
    scale = HEAD_DIM ** (-0.5)
    lanes = lax.broadcasted_iota(jnp.int32, (64, 192), 1)
    first = lanes < HEAD_DIM
    nothing = jnp.zeros((64, 192), BF16)

    def masked(rows_in):
        wide = rows_in.astype(F32)
        return jnp.concatenate(
            [jnp.where(first, wide, 0.0), jnp.where(first, 0.0, wide)], axis=0
        ).astype(BF16)

    blank = jnp.concatenate([nothing, nothing], axis=0)
    packed = jnp.concatenate(
        [
            jnp.concatenate([masked(query_pooled), blank], axis=1),
            jnp.concatenate([blank, masked(d_attended)], axis=1),
        ],
        axis=0,
    )
    products = dot_nt(packed, rows_kv)
    exp_scores = jnp.exp(products[:128] * scale)
    row_total = jnp.sum(exp_scores, axis=-1, keepdims=True)
    attn_probs = (exp_scores / row_total).astype(BF16)
    dprobs = products[128:]
    probs_wide = attn_probs.astype(F32)
    row_delta = jnp.sum(probs_wide * dprobs, axis=-1, keepdims=True)
    d_scores = (scale * probs_wide * (dprobs - row_delta)).astype(BF16)
    both = jnp.concatenate([d_scores, attn_probs], axis=0)
    rows_grad = dot_tn(both, packed).astype(BF16).reshape(16, 64, 384)
    mixed = dot_nn(both, rows_kv)
    from_keys, from_values = mixed[:128, :192], mixed[128:, 192:]
    query_grad = jnp.where(first, from_keys[:64], from_keys[64:]) + d_attended.astype(F32)
    attended = (
        jnp.where(first, from_values[:64], from_values[64:]) + query_pooled.astype(F32)
    ).astype(BF16)
    return rows_grad, query_grad, attended


def cut(rows_in):
    return [rows_in[:, i : i + 128] for i in range(0, rows_in.shape[1], 128)]


def after(query_grad, attended, normed, query_pool, held_cotangent, proj_weight):
    d_queries = spread_queries(query_grad, query_pool).astype(BF16)
    pieces = cut(dot_tn(d_queries, normed)) + cut(dot_tn(attended, held_cotangent))
    natural = dot_nn(selector(64, query_of, True), attended).astype(BF16)
    head_part = dot_nn(natural, proj_weight).astype(BF16)
    return jnp.stack(pieces).astype(BF16), d_queries, head_part


def weights(parts, normed, d_queries, key_pool, value_pool, qkv_weight, pieces):
    total = sum_four([parts[k] for k in range(4)])
    d_keys = spread_keys(total[:, :192], key_pool).astype(BF16)
    d_values = spread_keys(total[:, 192:], value_pool).astype(BF16)
    more = jnp.stack(cut(dot_tn(d_keys, normed)) + cut(dot_tn(d_values, normed))).astype(BF16)
    blank = jnp.zeros((1, 192, 128), BF16)
    d_normed = dot_nn(d_queries, qkv_weight[0])
    d_normed = d_normed + dot_nn(d_keys, qkv_weight[1])
    d_normed = d_normed + dot_nn(d_values, qkv_weight[2])
    return jnp.concatenate([pieces, more, blank], axis=0), d_normed.astype(BF16)


def finish(pieces):
    wide = pieces.astype(F32)

    def join(start, count):
        return jnp.concatenate([wide[start + i] for i in range(count)], axis=1)

    qkv_grad = jnp.stack([join(0, 3), join(9, 3), join(12, 3)])
    return qkv_grad, join(3, 6)


def back(sum_a, sum_b, held, ln_gain):
    total = sum_a.astype(F32) + sum_b.astype(F32)
    unit, inv_std = normalize(held.astype(F32))
    scaled = total[:128] * ln_gain
    grad = inv_std * (
        scaled
        - jnp.mean(scaled, axis=-1, keepdims=True)
        - unit * jnp.mean(scaled * unit, axis=-1, keepdims=True)
    )
    pooled = total[128:160] * 0.25
    spread = []
    for block in range(8):
        place = (block % 4) // 2
        spread.append(pooled[16 * place : 16 * place + 16])
    return ((grad + jnp.concatenate(spread, axis=0)).astype(BF16),)


def unpermute(rows_in):
    return (dot_nn(selector(256, token_of, True), rows_in).astype(BF16),)


def local(
    tokens,
    ln_gain,
    qkv_weight,
    query_pool,
    key_pool,
    value_pool,
    proj_weight,
    skip_weight,
    cotangent,
):
    core, half = lax.axis_index("core"), lax.axis_index("half")
    gain = ln_gain.reshape(1, -1)

    def pick(stacked, place, axis=0):
        return lax.dynamic_index_in_dim(stacked, place, axis, keepdims=False)

    other = swap(cotangent, "core")
    pair = jnp.where(
        core == 0,
        jnp.concatenate([cotangent, other], axis=1),
        jnp.concatenate([other, cotangent], axis=1),
    )
    far = swap(pair, "half")
    full_cotangent = jnp.where(
        half == 0, jnp.concatenate([pair, far], axis=1), jnp.concatenate([far, pair], axis=1)
    )

    own_kv, normed, held = fuse(
        front, [((16, 384), BF16), ((256, 384), BF16), ((256, 384), BF16)], "front"
    )(tokens, gain, qkv_weight, key_pool, value_pool)
    line_kv = jnp.concatenate([own_kv] + [shift(own_kv, "z", k) for k in (1, 2, 3)], axis=0)
    rows_kv = gather_plane(line_kv)

    query_pooled, d_attended, held_cotangent, skipped, d_pooled = fuse(
        middle,
        [
            ((64, 192), BF16),
            ((64, 192), BF16),
            ((64, 768), BF16),
            ((64, 192), F32),
            ((64, 384), BF16),
        ],
        "middle",
    )(normed, held, qkv_weight, query_pool, full_cotangent, cotangent, proj_weight, skip_weight)

    rows_grad, query_grad, attended = fuse(
        attend, [((16, 64, 384), BF16), ((64, 192), F32), ((64, 192), BF16)], "attend"
    )(rows_kv, query_pooled, d_attended)

    arrived = exchange_plane(rows_grad)
    line = jnp.sum(arrived.astype(F32), axis=0).astype(BF16).reshape(4, 16, 384)
    parts = jnp.stack([line[0]] + [shift(line[k], "z", -k) for k in (1, 2, 3)])

    pieces, d_queries, head_part = fuse(
        after, [((9, 192, 128), BF16), ((256, 192), BF16), ((64, 768), BF16)], "after"
    )(query_grad, attended, normed, query_pool, held_cotangent, proj_weight)

    pieces, d_normed = fuse(weights, [((16, 192, 128), BF16), ((256, 384), BF16)], "weights")(
        parts, normed, d_queries, key_pool, value_pool, qkv_weight, pieces
    )

    quarters = head_part.reshape(64, 2, 2, 192)

    def for_core(place):
        rows_out = pick(quarters, place, 2).reshape(64, 384)
        return jnp.concatenate(
            [
                pick(d_normed.reshape(2, 128, 384), place),
                pick(d_pooled.reshape(2, 32, 384), place),
                rows_out,
            ],
            axis=0,
        )

    both = (
        for_core(core).astype(F32) + swap(for_core(1 - core), "core").astype(F32)
    ).astype(BF16)
    rows_out = both[160:].reshape(64, 2, 192)
    sent = jnp.concatenate(
        [both[:160], pick(rows_out, 1 - half, 1).reshape(32, 384)], axis=0
    )
    taken = swap(sent, "half")

    reduced = jnp.sum(exchange_plane(pieces).astype(F32), axis=0).astype(BF16)
    reduced = sum_four([reduced] + [shift(reduced, "z", k) for k in (1, 2, 3)]).astype(BF16)
    qkv_grad, proj_grad = fuse(finish, [((3, 192, 384), F32), ((192, 768), F32)], "finish")(
        gather_plane(reduced)
    )

    summed = pick(rows_out, half, 1).astype(F32) + taken[160:].reshape(64, 192).astype(F32)
    block_out = (summed + skipped).astype(BF16)
    (own_rows,) = fuse(back, [((128, 384), BF16)], "back")(
        both[:160], taken[:160], pick(held.reshape(2, 128, 384), core), gain
    )
    other_rows = swap(own_rows, "core")
    ordered = jnp.where(
        core == 0,
        jnp.concatenate([own_rows, other_rows]),
        jnp.concatenate([other_rows, own_rows]),
    )
    (input_grad,) = fuse(unpermute, [((256, 384), BF16)], "unpermute")(ordered)
    return (block_out, input_grad, qkv_grad, proj_grad)


def solution(mesh):
    grid = Mesh(
        np.asarray(mesh.devices).reshape(4, 4, 4, 2, 2), ("y", "z", "x", "half", "core")
    )
    placed = (
        P(TILE, None),
        P(),
        P(None, HEAD, None),
        P(None, HEAD),
        P(None, HEAD),
        P(None, HEAD),
        P(HEAD, None),
        P(HEAD, None),
        P(TILE, HEAD),
    )
    return jax.shard_map(
        local,
        mesh=grid,
        in_specs=placed,
        out_specs=(P(TILE, HEAD), P(TILE, None), P(None, HEAD, None), P(HEAD, None)),
        check_vma=False,
    )
```

```python
import numpy as np

import jax
import jax.numpy as jnp
from jax import lax
from jax.experimental import pallas as pl
from jax.experimental.pallas import tpu as pltpu
from jax.sharding import Mesh
from jax.sharding import PartitionSpec as P

HEAD_DIM = 96
EPSILON = 1e-06
F32 = jnp.float32
BF16 = jnp.bfloat16
TILE = ("y", "z", "x")
HEAD = ("half", "core")
PLANE = ("y", "x")


def shift(block, axis, step):
    return lax.ppermute(block, axis, [(i, (i + step) % 4) for i in range(4)])


def swap(block, axis):
    return lax.ppermute(block, axis, [(0, 1), (1, 0)])


def swap_pair(block):
    return lax.ppermute(block, "z", [(i, i ^ 1) for i in range(4)])


def exchange(blocks, axes):
    return lax.all_to_all(blocks, axes, 0, 0, tiled=True)


def sum_four(parts):
    wide = [p.astype(F32) for p in parts]
    return (wide[0] + wide[2]) + (wide[1] + wide[3])


def fuse(function, outs, name, direct=False, flops=None):
    def call(*operands):
        count, stored = len(operands), len(outs)

        def kernel(*refs):
            sources, targets = refs[:count], refs[count : count + stored]
            if direct:
                held = refs[count + stored : -1]
                fetches = [
                    pltpu.make_async_copy(source, target, refs[-1].at[i])
                    for i, (source, target) in enumerate(zip(sources, held))
                ]
                for fetch in fetches:
                    fetch.start()
                for fetch in fetches:
                    fetch.wait()
                sources = held
            results = function(*[ref[...] for ref in sources])
            for ref, result in zip(targets, results):
                ref[...] = result

        scratch = []
        if direct:
            scratch = [pltpu.VMEM(x.shape, x.dtype) for x in operands]
            scratch.append(pltpu.SemaphoreType.DMA((count,)))
        return pl.pallas_call(
            kernel,
            out_shape=[jax.ShapeDtypeStruct(shape, dtype) for shape, dtype in outs],
            in_specs=[pl.BlockSpec(memory_space=pl.ANY if direct else pltpu.VMEM)] * count,
            out_specs=[pl.BlockSpec(memory_space=pltpu.VMEM)] * stored,
            scratch_shapes=scratch,
            compiler_params=pltpu.CompilerParams(vmem_limit_bytes=(60 if direct else 32) * 1024 * 1024),
            cost_estimate=flops
            and pl.CostEstimate(flops=flops, bytes_accessed=0, transcendentals=0),
            name=name,
        )(*operands)

    return call


def either(which, first, second):
    return jnp.where(which == 0, first, second)


def dot(a, b, contract):
    return lax.dot_general(a, b, (contract, ((), ())), preferred_element_type=F32)


def dot_nn(a, b):
    return dot(a, b, ((1,), (0,)))


def dot_nt(a, b):
    return dot(a, b, ((1,), (1,)))


def dot_tn(a, b):
    return dot(a, b, ((0,), (0,)))


def token_of(place):
    a, b, r, c = place >> 6, (place >> 4) & 3, (place >> 3) & 1, place & 7
    return (4 * r + a) * 32 + 4 * c + b


def query_of(place):
    a, b, r, c = place >> 5, (place >> 4) & 1, (place >> 3) & 1, place & 7
    return (2 * r + a) * 16 + 2 * c + b


def selector(count, source, transposed):
    rows = lax.broadcasted_iota(jnp.int32, (count, count), 0)
    columns = lax.broadcasted_iota(jnp.int32, (count, count), 1)
    hit = source(columns) == rows if transposed else source(rows) == columns
    return jnp.where(hit, 1.0, 0.0).astype(BF16)


def normalize(values_in):
    center = values_in - jnp.mean(values_in, axis=-1, keepdims=True)
    inv_std = lax.rsqrt(jnp.mean(center * center, axis=-1, keepdims=True) + EPSILON)
    return center * inv_std, inv_std


def pool_keys(feature, weight):
    wide = weight.astype(F32)
    total = wide[0:1] * feature[0:16]
    for k in range(1, 16):
        total = total + wide[k : k + 1] * feature[16 * k : 16 * k + 16]
    return total


def spread_keys(upstream, weight):
    wide = weight.astype(F32)
    return jnp.concatenate([wide[k : k + 1] * upstream for k in range(16)], axis=0)


def query_blocks():
    out = []
    for a2 in range(2):
        for b2 in range(2):
            out.append(
                [
                    (2 * a1 + b1, (2 * a2 + a1) * 4 + 2 * b2 + b1)
                    for a1 in range(2)
                    for b1 in range(2)
                ]
            )
    return out


def pool_queries(feature, weight):
    wide = weight.astype(F32)
    rows = []
    for members in query_blocks():
        total = None
        for tap, block in members:
            term = feature[16 * block : 16 * block + 16]
            if weight is not None:
                term = wide[tap : tap + 1] * term
            total = term if total is None else total + term
        rows.append(total)
    return jnp.concatenate(rows, axis=0)


def spread_queries(upstream, weight):
    wide = weight.astype(F32)
    blocks = [None] * 16
    for place, members in enumerate(query_blocks()):
        for tap, block in members:
            blocks[block] = wide[tap : tap + 1] * upstream[16 * place : 16 * place + 16]
    return jnp.concatenate(blocks, axis=0)


def front(tokens, ln_gain, weight_kv, key_pool, value_pool):
    held = dot_nn(selector(256, token_of, False), tokens)
    unit, _ = normalize(held)
    normed = (unit * ln_gain[None, :]).astype(BF16)
    key_pooled = pool_keys(dot_nt(normed, weight_kv[1]), key_pool)
    value_pooled = pool_keys(dot_nt(normed, weight_kv[2]), value_pool)
    odd = lax.rem(lax.axis_index("z"), 2)
    blank = jnp.zeros((16, 64), F32)
    rows = [
        jnp.concatenate([key_pooled[:, part], value_pooled[:, part], blank], axis=1)
        for part in (slice(0, HEAD_DIM), slice(HEAD_DIM, 2 * HEAD_DIM))
    ]
    same = either(odd, rows[0], rows[1]).astype(BF16)
    other = either(odd, rows[1], rows[0]).astype(BF16)
    return same, other, normed, held.astype(BF16)


def fold_rows(rows_in):
    count = rows_in.shape[0] // 2
    return jnp.concatenate([rows_in[:count, :192], rows_in[count:, :192]], axis=1)


def unfold_rows(rows_in):
    return jnp.concatenate([rows_in[:, :192], rows_in[:, 192:]], axis=0)


def copy_line(part_0, part_1, part_2, part_3):
    line = jnp.concatenate([part_0, part_1, part_2, part_3], axis=0)
    line = fold_rows(line.astype(F32)).astype(BF16)
    return (jnp.broadcast_to(line[None], (16, 32, 384)),)


def middle(
    normed, held, weight_q, query_pool, cot_0, cot_1, cot_2, cot_3, proj_weight, skip_weight
):
    core, half = lax.axis_index("core"), lax.axis_index("half")
    pairs = [
        jnp.concatenate([either(core, p, q), either(core, q, p)], axis=1)
        for p, q in ((cot_0.astype(F32), cot_1.astype(F32)), (cot_2.astype(F32), cot_3.astype(F32)))
    ]
    full_cotangent = jnp.concatenate(
        [either(half, pairs[0], pairs[1]), either(half, pairs[1], pairs[0])], axis=1
    ).astype(BF16)
    query_pooled = pool_queries(dot_nt(normed, weight_q[0]), query_pool).astype(BF16)
    to_held = selector(64, query_of, False)
    held_cotangent = dot_nn(to_held, full_cotangent).astype(BF16)
    d_attended = dot_nt(held_cotangent, proj_weight).astype(BF16)
    ones = jnp.ones((4, held.shape[1]), F32)
    pooled_input = (pool_queries(held.astype(F32), ones) * 0.25).astype(BF16)
    natural = dot_nn(selector(64, query_of, True), pooled_input).astype(BF16)
    skipped = dot_nt(natural, skip_weight)
    own_cotangent = dot_nn(to_held, cot_0).astype(BF16)
    d_pooled = dot_nn(own_cotangent, skip_weight).astype(BF16)
    blank = jnp.zeros((64, 64), F32)
    queries, grads = query_pooled.astype(F32), d_attended.astype(F32)
    rows = [
        jnp.concatenate([queries[:, part], grads[:, part], blank], axis=1)
        for part in (slice(0, HEAD_DIM), slice(HEAD_DIM, 2 * HEAD_DIM))
    ]
    odd = lax.rem(lax.axis_index("z"), 2)
    mine = either(odd, rows[0], rows[1]).astype(BF16)
    theirs = either(odd, rows[1], rows[0]).astype(BF16)
    return mine, theirs, held_cotangent, skipped, d_pooled


def attend(rows_kv, mine, received):
    rows_kv = unfold_rows(rows_kv.reshape(512, 384))
    scale = HEAD_DIM ** (-0.5)
    wide = jnp.concatenate([mine, received], axis=0).astype(F32)[:, :192]
    lanes = lax.broadcasted_iota(jnp.int32, (128, 192), 1)
    on_keys = lanes < HEAD_DIM
    packed = jnp.concatenate(
        [jnp.where(on_keys, wide, 0.0), jnp.where(on_keys, 0.0, wide)], axis=0
    ).astype(BF16)
    products = dot_nt(packed, rows_kv)
    exp_scores = jnp.exp(products[:128] * scale)
    row_total = jnp.sum(exp_scores, axis=-1, keepdims=True)
    attn_probs = (exp_scores / row_total).astype(BF16)
    dprobs = products[128:]
    probs_wide = attn_probs.astype(F32)
    row_delta = jnp.sum(probs_wide * dprobs, axis=-1, keepdims=True)
    d_scores = (scale * probs_wide * (dprobs - row_delta)).astype(BF16)
    both = jnp.concatenate([d_scores, attn_probs], axis=0)
    rows_grad = fold_rows(dot_tn(both, packed)).astype(BF16).reshape(16, 32, 384)
    mixed = dot_nn(both, rows_kv)
    mixed = jnp.where(on_keys, mixed[:128], mixed[128:])
    mixed = mixed + jnp.concatenate([wide[:, HEAD_DIM:], wide[:, :HEAD_DIM]], axis=1)
    mixed = jnp.concatenate([mixed, jnp.zeros((128, 64), F32)], axis=1)
    return rows_grad, mixed[:64], mixed[64:].astype(BF16)


def cut(rows_in):
    return [rows_in[:, i : i + 128] for i in range(0, rows_in.shape[1], 128)]


def after(mixed, returned, normed, query_pool, held_cotangent, proj_weight):
    odd = lax.rem(lax.axis_index("z"), 2)
    returned = returned.astype(F32)
    first, second = either(odd, mixed, returned), either(odd, returned, mixed)
    query_grad = jnp.concatenate([first[:, :HEAD_DIM], second[:, :HEAD_DIM]], axis=1)
    attended = jnp.concatenate(
        [first[:, HEAD_DIM : 2 * HEAD_DIM], second[:, HEAD_DIM : 2 * HEAD_DIM]], axis=1
    ).astype(BF16)
    d_queries = spread_queries(query_grad, query_pool).astype(BF16)
    pieces = cut(dot_tn(d_queries, normed)) + cut(dot_tn(attended, held_cotangent))
    natural = dot_nn(selector(64, query_of, True), attended).astype(BF16)
    head_part = dot_nn(natural, proj_weight).astype(BF16)
    return jnp.stack(pieces).astype(BF16), d_queries, head_part


def weights(
    part_0,
    part_1,
    part_2,
    part_3,
    normed,
    d_queries,
    key_pool,
    value_pool,
    qkv_weight,
    pieces,
    d_pooled,
    head_part,
):
    core, odd = lax.axis_index("core"), lax.rem(lax.axis_index("z"), 2)
    same = part_0.astype(F32) + part_2.astype(F32)
    other = part_1.astype(F32) + part_3.astype(F32)
    per_head = [either(odd, same, other), either(odd, other, same)]
    key_grad = jnp.concatenate([t[:, :HEAD_DIM] for t in per_head], axis=1)
    value_grad = jnp.concatenate([t[:, HEAD_DIM : 2 * HEAD_DIM] for t in per_head], axis=1)
    d_keys = spread_keys(key_grad, key_pool).astype(BF16)
    d_values = spread_keys(value_grad, value_pool).astype(BF16)
    more = jnp.stack(cut(dot_tn(d_keys, normed)) + cut(dot_tn(d_values, normed))).astype(BF16)
    blank = jnp.zeros((1, 192, 128), BF16)
    d_normed = dot_nn(d_queries, qkv_weight[0])
    d_normed = d_normed + dot_nn(d_keys, qkv_weight[1])
    d_normed = d_normed + dot_nn(d_values, qkv_weight[2])
    pooled, rows = d_pooled.astype(F32), head_part.astype(F32)
    loads = []
    for c in range(2):
        channels = [rows[:, 192 * (2 * p + c) : 192 * (2 * p + c) + 192] for p in range(2)]
        loads.append(
            jnp.concatenate(
                [
                    d_normed[128 * c : 128 * c + 128],
                    pooled[32 * c : 32 * c + 32],
                    jnp.concatenate(channels, axis=1),
                ],
                axis=0,
            )
        )
    kept = either(core, loads[0], loads[1]).astype(BF16)
    sent = either(core, loads[1], loads[0]).astype(BF16)
    return jnp.concatenate([pieces, more, blank], axis=0), kept, sent


def settle(part_0, part_1, part_2, part_3):
    total = sum_four([part_0, part_1, part_2, part_3]).astype(BF16)
    return (jnp.broadcast_to(total[None], (16, *total.shape)),)


def line_sum(arrived):
    total = arrived[0].astype(F32)
    for source in range(1, 16):
        total = total + arrived[source].astype(F32)
    line = unfold_rows(total)
    line = jnp.concatenate([line, jnp.zeros((64, 64), F32)], axis=1).astype(BF16)
    return tuple(line[16 * k : 16 * k + 16] for k in range(4))


def finish(pieces):
    wide = pieces.astype(F32)

    def join(start, count):
        return jnp.concatenate([wide[start + i] for i in range(count)], axis=1)

    qkv_grad = jnp.stack([join(0, 3), join(9, 3), join(12, 3)])
    return qkv_grad, join(3, 6)


def mix(kept, received):
    half = lax.axis_index("half")
    both = kept.astype(F32) + received.astype(F32)
    rows = [both[160:, :192], both[160:, 192:]]
    leaving = either(half, rows[1], rows[0])
    staying = either(half, rows[0], rows[1])
    folded = jnp.concatenate([leaving[:32], leaving[32:]], axis=1)
    return both[:160].astype(BF16), jnp.concatenate([both[:160], folded], axis=0).astype(BF16), staying


def back(both, taken, staying, skipped, held, ln_gain):
    core = lax.axis_index("core")
    total = both.astype(F32) + taken[:160].astype(F32)
    held = held.astype(F32)
    unit, inv_std = normalize(either(core, held[:128], held[128:]))
    scaled = total[:128] * ln_gain[None, :]
    grad = inv_std * (
        scaled
        - jnp.mean(scaled, axis=-1, keepdims=True)
        - unit * jnp.mean(scaled * unit, axis=-1, keepdims=True)
    )
    pooled = total[128:160] * 0.25
    grown = []
    for block in range(8):
        half = (block % 4) // 2
        grown.append(pooled[16 * half : 16 * half + 16])
    folded = taken[160:].astype(F32)
    arrived = jnp.concatenate([folded[:, :192], folded[:, 192:]], axis=0)
    block_out = (staying + arrived + skipped).astype(BF16)
    return (grad + jnp.concatenate(grown, axis=0)).astype(BF16), block_out


def unpermute(own_rows, other_rows):
    core = lax.axis_index("core")
    own_rows, other_rows = own_rows.astype(F32), other_rows.astype(F32)
    ordered = jnp.concatenate(
        [either(core, own_rows, other_rows), either(core, other_rows, own_rows)], axis=0
    ).astype(BF16)
    return (dot_nn(selector(256, token_of, True), ordered).astype(BF16),)


def local(
    tokens,
    ln_gain,
    qkv_weight,
    query_pool,
    key_pool,
    value_pool,
    proj_weight,
    skip_weight,
    cotangent,
):
    cot_far = swap(cotangent, "half")
    cot_near = swap(cotangent, "core")

    same_kv, other_kv, normed, held = fuse(
        front,
        [((16, 256), BF16)] * 2 + [((256, 384), BF16)] * 2,
        "front",
        direct=True,
    )(tokens, ln_gain, qkv_weight, key_pool, value_pool)
    line_kv = [same_kv, shift(other_kv, "z", 1), shift(same_kv, "z", 2), shift(other_kv, "z", 3)]
    line_kv, cot_far = lax.optimization_barrier((line_kv, cot_far))
    cot_both = swap(cot_far, "core")
    (copies_kv,) = fuse(copy_line, [((16, 32, 384), BF16)], "copy_line")(*line_kv)
    rows_kv = exchange(copies_kv, PLANE)

    mine, theirs, held_cotangent, skipped, d_pooled = fuse(
        middle,
        [
            ((64, 256), BF16),
            ((64, 256), BF16),
            ((64, 768), BF16),
            ((64, 192), F32),
            ((64, 384), BF16),
        ],
        "middle",
    )(
        normed,
        held,
        qkv_weight,
        query_pool,
        cotangent,
        cot_near,
        cot_far,
        cot_both,
        proj_weight,
        skip_weight,
    )
    rows_grad, mixed, returned = fuse(
        attend, [((16, 32, 384), BF16), ((64, 256), F32), ((64, 256), BF16)], "attend"
    )(rows_kv, mine, swap_pair(theirs))

    arrived = exchange(rows_grad, PLANE)
    line = fuse(line_sum, [((16, 256), BF16)] * 4, "line_sum")(arrived)
    parts = [line[0]] + [shift(line[k], "z", -k) for k in (1, 2, 3)]
    pieces, d_queries, head_part = fuse(
        after, [((9, 192, 128), BF16), ((256, 192), BF16), ((64, 768), BF16)], "after"
    )(mixed, swap_pair(returned), normed, query_pool, held_cotangent, proj_weight)

    pieces, kept, sent = fuse(
        weights,
        [((16, 192, 128), BF16), ((224, 384), BF16), ((224, 384), BF16)],
        "weights",
    )(
        *parts,
        normed,
        d_queries,
        key_pool,
        value_pool,
        qkv_weight,
        pieces,
        d_pooled,
        head_part,
    )

    both, sent, staying = fuse(
        mix, [((160, 384), BF16), ((192, 384), BF16), ((64, 192), F32)], "mix"
    )(kept, swap(sent, "core"))
    taken = swap(sent, "half")

    reduced = jnp.sum(exchange(pieces, PLANE).astype(F32), axis=0).astype(BF16)
    reduced, both = lax.optimization_barrier((reduced, both))
    (copies,) = fuse(settle, [((16, 192, 128), BF16)], "settle")(
        reduced, *[shift(reduced, "z", k) for k in (1, 2, 3)]
    )
    qkv_grad, proj_grad = fuse(finish, [((3, 192, 384), F32), ((192, 768), F32)], "finish")(
        exchange(copies, PLANE)
    )

    own_rows, block_out = fuse(back, [((128, 384), BF16), ((64, 192), BF16)], "back", flops=8 * 10**9)(
        both, taken, staying, skipped, held, ln_gain
    )
    (input_grad,) = fuse(unpermute, [((256, 384), BF16)], "unpermute")(
        own_rows, swap(own_rows, "core")
    )
    return (block_out, input_grad, qkv_grad, proj_grad)


def solution(mesh):
    grid = Mesh(
        np.asarray(mesh.devices).reshape(4, 4, 4, 2, 2), ("y", "z", "x", "half", "core")
    )
    placed = (
        P(TILE, None),
        P(),
        P(None, HEAD, None),
        P(None, HEAD),
        P(None, HEAD),
        P(None, HEAD),
        P(HEAD, None),
        P(HEAD, None),
        P(TILE, HEAD),
    )
    return jax.shard_map(
        local,
        mesh=grid,
        in_specs=placed,
        out_specs=(P(TILE, HEAD), P(TILE, None), P(None, HEAD, None), P(HEAD, None)),
        check_vma=False,
    )
```

```python
import numpy as np

import jax
import jax.numpy as jnp
from jax import lax
from jax.experimental import pallas as pl
from jax.experimental.pallas import tpu as pltpu
from jax.sharding import Mesh
from jax.sharding import PartitionSpec as P

HEAD_DIM = 96
EPSILON = 1e-06
F32 = jnp.float32
BF16 = jnp.bfloat16
TILE = ("y", "z", "x")
HEAD = ("half", "core")
PLANE = ("y", "x")


def shift(block, axis, step):
    return lax.ppermute(block, axis, [(i, (i + step) % 4) for i in range(4)])


def swap(block, axis):
    return lax.ppermute(block, axis, [(0, 1), (1, 0)])


def swap_z(block, bit):
    return lax.ppermute(block, "z", [(i, i ^ bit) for i in range(4)])


def exchange_pairs(blocks):
    groups = [
        [16 * y + 4 * z + x for y in range(4) for z in (first, first + 1) for x in range(4)]
        for first in (0, 2)
    ]
    return lax.all_to_all(blocks, TILE, 0, 0, tiled=True, axis_index_groups=groups)


def exchange(blocks, axes):
    return lax.all_to_all(blocks, axes, 0, 0, tiled=True)


def sum_four(parts):
    wide = [p.astype(F32) for p in parts]
    return (wide[0] + wide[2]) + (wide[1] + wide[3])


def fuse(function, outs, name, direct=False, flops=None):
    def call(*operands):
        count, stored = len(operands), len(outs)

        def kernel(*refs):
            sources, targets = refs[:count], refs[count : count + stored]
            if direct:
                held = refs[count + stored : -1]
                fetches = [
                    pltpu.make_async_copy(source, target, refs[-1].at[i])
                    for i, (source, target) in enumerate(zip(sources, held))
                ]
                for fetch in fetches:
                    fetch.start()
                for fetch in fetches:
                    fetch.wait()
                sources = held
            results = function(*[ref[...] for ref in sources])
            for ref, result in zip(targets, results):
                ref[...] = result

        scratch = []
        if direct:
            scratch = [pltpu.VMEM(x.shape, x.dtype) for x in operands]
            scratch.append(pltpu.SemaphoreType.DMA((count,)))
        return pl.pallas_call(
            kernel,
            out_shape=[jax.ShapeDtypeStruct(shape, dtype) for shape, dtype in outs],
            in_specs=[pl.BlockSpec(memory_space=pl.ANY if direct else pltpu.VMEM)] * count,
            out_specs=[pl.BlockSpec(memory_space=pltpu.VMEM)] * stored,
            scratch_shapes=scratch,
            compiler_params=pltpu.CompilerParams(vmem_limit_bytes=(60 if direct else 32) * 1024 * 1024),
            cost_estimate=flops
            and pl.CostEstimate(flops=flops, bytes_accessed=0, transcendentals=0),
            name=name,
        )(*operands)

    return call


def either(which, first, second):
    return jnp.where(which == 0, first, second)


def dot(a, b, contract):
    return lax.dot_general(a, b, (contract, ((), ())), preferred_element_type=F32)


def dot_nn(a, b):
    return dot(a, b, ((1,), (0,)))


def dot_nt(a, b):
    return dot(a, b, ((1,), (1,)))


def dot_tn(a, b):
    return dot(a, b, ((0,), (0,)))


def token_of(place):
    a, b, r, c = place >> 6, (place >> 4) & 3, (place >> 3) & 1, place & 7
    return (4 * r + a) * 32 + 4 * c + b


def query_of(place):
    a, b, r, c = place >> 5, (place >> 4) & 1, (place >> 3) & 1, place & 7
    return (2 * r + a) * 16 + 2 * c + b


def selector(count, source, transposed):
    rows = lax.broadcasted_iota(jnp.int32, (count, count), 0)
    columns = lax.broadcasted_iota(jnp.int32, (count, count), 1)
    hit = source(columns) == rows if transposed else source(rows) == columns
    return jnp.where(hit, 1.0, 0.0).astype(BF16)


def normalize(values_in):
    center = values_in - jnp.mean(values_in, axis=-1, keepdims=True)
    inv_std = lax.rsqrt(jnp.mean(center * center, axis=-1, keepdims=True) + EPSILON)
    return center * inv_std, inv_std


def pool_keys(feature, weight):
    wide = weight.astype(F32)
    total = wide[0:1] * feature[0:16]
    for k in range(1, 16):
        total = total + wide[k : k + 1] * feature[16 * k : 16 * k + 16]
    return total


def spread_keys(upstream, weight):
    wide = weight.astype(F32)
    return jnp.concatenate([wide[k : k + 1] * upstream for k in range(16)], axis=0)


def query_blocks():
    out = []
    for a2 in range(2):
        for b2 in range(2):
            out.append(
                [
                    (2 * a1 + b1, (2 * a2 + a1) * 4 + 2 * b2 + b1)
                    for a1 in range(2)
                    for b1 in range(2)
                ]
            )
    return out


def pool_queries(feature, weight):
    wide = weight.astype(F32)
    rows = []
    for members in query_blocks():
        total = None
        for tap, block in members:
            term = feature[16 * block : 16 * block + 16]
            if weight is not None:
                term = wide[tap : tap + 1] * term
            total = term if total is None else total + term
        rows.append(total)
    return jnp.concatenate(rows, axis=0)


def spread_queries(upstream, weight):
    wide = weight.astype(F32)
    blocks = [None] * 16
    for place, members in enumerate(query_blocks()):
        for tap, block in members:
            blocks[block] = wide[tap : tap + 1] * upstream[16 * place : 16 * place + 16]
    return jnp.concatenate(blocks, axis=0)


def front(tokens, ln_gain, weight_kv, key_pool, value_pool):
    held = dot_nn(selector(256, token_of, False), tokens)
    unit, _ = normalize(held)
    normed = (unit * ln_gain[None, :]).astype(BF16)
    key_pooled = pool_keys(dot_nt(normed, weight_kv[1]), key_pool)
    value_pooled = pool_keys(dot_nt(normed, weight_kv[2]), value_pool)
    blank = jnp.zeros((16, 64), F32)
    rows = [
        jnp.concatenate([key_pooled[:, part], value_pooled[:, part], blank], axis=1)
        for part in (slice(0, HEAD_DIM), slice(HEAD_DIM, 2 * HEAD_DIM))
    ]
    rows = jnp.concatenate(rows, axis=0).astype(BF16)
    return rows, rows, normed, held.astype(BF16)


def fold_rows(rows_in):
    count = rows_in.shape[0] // 2
    return jnp.concatenate([rows_in[:count, :192], rows_in[count:, :192]], axis=1)


def unfold_rows(rows_in):
    return jnp.concatenate([rows_in[:, :192], rows_in[:, 192:]], axis=0)


def copy_pair(own, other):
    wide, other = own.astype(F32), other.astype(F32)
    heads = [
        fold_rows(jnp.concatenate([wide[start : start + 16], other[start : start + 16]], axis=0))
        for start in (0, 16)
    ]
    heads = jnp.concatenate([jnp.broadcast_to(h[None, None], (1, 4, 16, 384)) for h in heads])
    return (jnp.broadcast_to(heads[None], (4, 2, 4, 16, 384)).astype(BF16).reshape(32, 16, 384),)


def middle(
    normed, held, weight_q, query_pool, cot_0, cot_1, cot_2, cot_3, proj_weight, skip_weight
):
    core, half = lax.axis_index("core"), lax.axis_index("half")
    pairs = [
        jnp.concatenate([either(core, p, q), either(core, q, p)], axis=1)
        for p, q in ((cot_0.astype(F32), cot_1.astype(F32)), (cot_2.astype(F32), cot_3.astype(F32)))
    ]
    full_cotangent = jnp.concatenate(
        [either(half, pairs[0], pairs[1]), either(half, pairs[1], pairs[0])], axis=1
    ).astype(BF16)
    query_pooled = pool_queries(dot_nt(normed, weight_q[0]), query_pool).astype(BF16)
    to_held = selector(64, query_of, False)
    held_cotangent = dot_nn(to_held, full_cotangent).astype(BF16)
    d_attended = dot_nt(held_cotangent, proj_weight).astype(BF16)
    ones = jnp.ones((4, held.shape[1]), F32)
    pooled_input = (pool_queries(held.astype(F32), ones) * 0.25).astype(BF16)
    natural = dot_nn(selector(64, query_of, True), pooled_input).astype(BF16)
    skipped = dot_nt(natural, skip_weight)
    own_cotangent = dot_nn(to_held, cot_0).astype(BF16)
    d_pooled = dot_nn(own_cotangent, skip_weight).astype(BF16)
    blank = jnp.zeros((64, 64), F32)
    queries, grads = query_pooled.astype(F32), d_attended.astype(F32)
    rows = [
        jnp.concatenate([queries[:, part], grads[:, part], blank], axis=1)
        for part in (slice(0, HEAD_DIM), slice(HEAD_DIM, 2 * HEAD_DIM))
    ]
    odd = lax.rem(lax.axis_index("z"), 2)
    mine = either(odd, rows[0], rows[1]).astype(BF16)
    theirs = either(odd, rows[1], rows[0]).astype(BF16)
    return mine, theirs, held_cotangent, skipped, d_pooled


def attend(rows_kv, mine, received):
    rows_kv = unfold_rows(rows_kv.reshape(512, 384))
    scale = HEAD_DIM ** (-0.5)
    wide = jnp.concatenate([mine, received], axis=0).astype(F32)[:, :192]
    lanes = lax.broadcasted_iota(jnp.int32, (128, 192), 1)
    on_keys = lanes < HEAD_DIM
    packed = jnp.concatenate(
        [jnp.where(on_keys, wide, 0.0), jnp.where(on_keys, 0.0, wide)], axis=0
    ).astype(BF16)
    products = dot_nt(packed, rows_kv)
    exp_scores = jnp.exp(products[:128] * scale)
    row_total = jnp.sum(exp_scores, axis=-1, keepdims=True)
    attn_probs = (exp_scores / row_total).astype(BF16)
    dprobs = products[128:]
    probs_wide = attn_probs.astype(F32)
    row_delta = jnp.sum(probs_wide * dprobs, axis=-1, keepdims=True)
    d_scores = (scale * probs_wide * (dprobs - row_delta)).astype(BF16)
    both = jnp.concatenate([d_scores, attn_probs], axis=0)
    rows_grad = fold_rows(dot_tn(both, packed)).astype(BF16).reshape(32, 16, 384)
    mixed = dot_nn(both, rows_kv)
    mixed = jnp.where(on_keys, mixed[:128], mixed[128:])
    mixed = mixed + jnp.concatenate([wide[:, HEAD_DIM:], wide[:, :HEAD_DIM]], axis=1)
    mixed = jnp.concatenate([mixed, jnp.zeros((128, 64), F32)], axis=1)
    return rows_grad, mixed[:64], mixed[64:].astype(BF16)


def cut(rows_in):
    return [rows_in[:, i : i + 128] for i in range(0, rows_in.shape[1], 128)]


def after(mixed, returned, normed, query_pool, held_cotangent, proj_weight):
    odd = lax.rem(lax.axis_index("z"), 2)
    returned = returned.astype(F32)
    first, second = either(odd, mixed, returned), either(odd, returned, mixed)
    query_grad = jnp.concatenate([first[:, :HEAD_DIM], second[:, :HEAD_DIM]], axis=1)
    attended = jnp.concatenate(
        [first[:, HEAD_DIM : 2 * HEAD_DIM], second[:, HEAD_DIM : 2 * HEAD_DIM]], axis=1
    ).astype(BF16)
    d_queries = spread_queries(query_grad, query_pool).astype(BF16)
    pieces = cut(dot_tn(d_queries, normed)) + cut(dot_tn(attended, held_cotangent))
    natural = dot_nn(selector(64, query_of, True), attended).astype(BF16)
    head_part = dot_nn(natural, proj_weight).astype(BF16)
    return jnp.stack(pieces).astype(BF16), d_queries, head_part


def tile_grads(own, other, key_pool, value_pool):
    total = own.astype(F32) + other.astype(F32)
    per_head = [total[:16], total[16:]]
    key_grad = jnp.concatenate([t[:, :HEAD_DIM] for t in per_head], axis=1)
    value_grad = jnp.concatenate([t[:, HEAD_DIM : 2 * HEAD_DIM] for t in per_head], axis=1)
    d_keys = spread_keys(key_grad, key_pool).astype(BF16)
    d_values = spread_keys(value_grad, value_pool).astype(BF16)
    return d_keys, d_values


def weights(own, other, normed, key_pool, value_pool, pieces):
    d_keys, d_values = tile_grads(own, other, key_pool, value_pool)
    more = jnp.stack(cut(dot_tn(d_keys, normed)) + cut(dot_tn(d_values, normed))).astype(BF16)
    blank = jnp.zeros((1, 192, 128), BF16)
    pieces = jnp.concatenate([pieces, more, blank], axis=0).reshape(32, 96, 128)
    return pieces, d_keys, d_values


def spread(d_keys, d_values, d_queries, qkv_weight, d_pooled, head_part):
    core = lax.axis_index("core")
    d_normed = dot_nn(d_queries, qkv_weight[0])
    d_normed = d_normed + dot_nn(d_keys, qkv_weight[1])
    d_normed = d_normed + dot_nn(d_values, qkv_weight[2])
    pooled, rows = d_pooled.astype(F32), head_part.astype(F32)
    loads = []
    for c in range(2):
        channels = [rows[:, 192 * (2 * p + c) : 192 * (2 * p + c) + 192] for p in range(2)]
        loads.append(
            jnp.concatenate(
                [
                    d_normed[128 * c : 128 * c + 128],
                    pooled[32 * c : 32 * c + 32],
                    jnp.concatenate(channels, axis=1),
                ],
                axis=0,
            )
        )
    kept = either(core, loads[0], loads[1]).astype(BF16)
    sent = either(core, loads[1], loads[0]).astype(BF16)
    return kept, sent


def settle(part_0, part_1):
    total = (part_0.astype(F32) + part_1.astype(F32)).astype(BF16)
    return (jnp.broadcast_to(total[None], (32, *total.shape)),)


def pair_sum(arrived):
    arrived = arrived.reshape(4, 2, 4, 16, 384)
    own, other = [], []
    blank = jnp.zeros((16, 64), F32)
    for h in range(2):
        total = None
        for y in range(4):
            for x in range(4):
                block = arrived[y, h, x].astype(F32)
                total = block if total is None else total + block
        own.append(jnp.concatenate([total[:, :192], blank], axis=1))
        other.append(jnp.concatenate([total[:, 192:], blank], axis=1))
    return jnp.concatenate(own, axis=0).astype(BF16), jnp.concatenate(other, axis=0).astype(BF16)


def finish(pieces):
    parts = [(0, 0), (1, 3), (1, 6), (0, 9), (0, 12)]

    def kernel(source, qkv_grad, proj_grad, room, semaphores):
        copies = []
        for i, (output, start) in enumerate(parts):
            for lane in range(3):
                piece = source[2 * (start + lane) : 2 * (start + lane) + 2].reshape(192, 128)
                room[i, :, 128 * lane : 128 * lane + 128] = piece.astype(F32)
            if output == 0:
                target = qkv_grad.at[(0, None, None, 1, 2)[i]]
            else:
                target = proj_grad.at[:, pl.ds(384 * (i - 1), 384)]
            copies.append(pltpu.make_async_copy(room.at[i], target, semaphores.at[i]))
            copies[-1].start()
        for copy in copies:
            copy.wait()

    return pl.pallas_call(
        kernel,
        out_shape=[
            jax.ShapeDtypeStruct((3, 192, 384), F32),
            jax.ShapeDtypeStruct((192, 768), F32),
        ],
        in_specs=[pl.BlockSpec(memory_space=pltpu.VMEM)],
        out_specs=[pl.BlockSpec(memory_space=pl.ANY)] * 2,
        scratch_shapes=[pltpu.VMEM((5, 192, 384), F32), pltpu.SemaphoreType.DMA((5,))],
        compiler_params=pltpu.CompilerParams(vmem_limit_bytes=32 * 1024 * 1024),
        name="finish",
    )(pieces)


def mix(kept, received):
    half = lax.axis_index("half")
    both = kept.astype(F32) + received.astype(F32)
    rows = [both[160:, :192], both[160:, 192:]]
    leaving = either(half, rows[1], rows[0])
    staying = either(half, rows[0], rows[1])
    folded = jnp.concatenate([leaving[:32], leaving[32:]], axis=1)
    return both[:160].astype(BF16), jnp.concatenate([both[:160], folded], axis=0).astype(BF16), staying


def back(both, taken, staying, skipped, held, ln_gain):
    core = lax.axis_index("core")
    total = both.astype(F32) + taken[:160].astype(F32)
    held = held.astype(F32)
    unit, inv_std = normalize(either(core, held[:128], held[128:]))
    scaled = total[:128] * ln_gain[None, :]
    grad = inv_std * (
        scaled
        - jnp.mean(scaled, axis=-1, keepdims=True)
        - unit * jnp.mean(scaled * unit, axis=-1, keepdims=True)
    )
    pooled = total[128:160] * 0.25
    grown = []
    for block in range(8):
        half = (block % 4) // 2
        grown.append(pooled[16 * half : 16 * half + 16])
    folded = taken[160:].astype(F32)
    arrived = jnp.concatenate([folded[:, :192], folded[:, 192:]], axis=0)
    block_out = (staying + arrived + skipped).astype(BF16)
    return (grad + jnp.concatenate(grown, axis=0)).astype(BF16), block_out


def unpermute(own_rows, other_rows):
    core = lax.axis_index("core")
    own_rows, other_rows = own_rows.astype(F32), other_rows.astype(F32)
    ordered = jnp.concatenate(
        [either(core, own_rows, other_rows), either(core, other_rows, own_rows)], axis=0
    ).astype(BF16)
    return (dot_nn(selector(256, token_of, True), ordered).astype(BF16),)


def local(
    tokens,
    ln_gain,
    qkv_weight,
    query_pool,
    key_pool,
    value_pool,
    proj_weight,
    skip_weight,
    cotangent,
):
    cot_far = swap(cotangent, "half")
    cot_near = swap(cotangent, "core")

    own_kv, sent_kv, normed, held = fuse(
        front,
        [((32, 256), BF16)] * 2 + [((256, 384), BF16)] * 2,
        "front",
        direct=True,
    )(tokens, ln_gain, qkv_weight, key_pool, value_pool)
    other_kv = swap_z(sent_kv, 2)
    other_kv, cot_far, cot_near = lax.optimization_barrier((other_kv, cot_far, cot_near))
    cot_both = swap(cot_far, "core")
    (copies_kv,) = fuse(copy_pair, [((32, 16, 384), BF16)], "copy_pair")(own_kv, other_kv)
    rows_kv = exchange_pairs(copies_kv)

    mine, theirs, held_cotangent, skipped, d_pooled = fuse(
        middle,
        [
            ((64, 256), BF16),
            ((64, 256), BF16),
            ((64, 768), BF16),
            ((64, 192), F32),
            ((64, 384), BF16),
        ],
        "middle",
    )(
        normed,
        held,
        qkv_weight,
        query_pool,
        cotangent,
        cot_near,
        cot_far,
        cot_both,
        proj_weight,
        skip_weight,
    )
    rows_grad, mixed, returned = fuse(
        attend, [((32, 16, 384), BF16), ((64, 256), F32), ((64, 256), BF16)], "attend"
    )(rows_kv, mine, swap_z(theirs, 1))

    arrived = exchange_pairs(rows_grad)
    own_grad, other_grad = fuse(pair_sum, [((32, 256), BF16)] * 2, "pair_sum")(arrived)
    other_grad = swap_z(other_grad, 2)
    pieces, d_queries, head_part = fuse(
        after, [((9, 192, 128), BF16), ((256, 192), BF16), ((64, 768), BF16)], "after"
    )(mixed, swap_z(returned, 1), normed, query_pool, held_cotangent, proj_weight)

    pieces, d_keys, d_values = fuse(
        weights, [((32, 96, 128), BF16)] + [((256, 192), BF16)] * 2, "weights"
    )(own_grad, other_grad, normed, key_pool, value_pool, pieces)
    arrived = exchange_pairs(pieces)
    kept, sent = fuse(spread, [((224, 384), BF16)] * 2, "spread")(
        d_keys, d_values, d_queries, qkv_weight, d_pooled, head_part
    )

    both, sent, staying = fuse(
        mix, [((160, 384), BF16), ((192, 384), BF16), ((64, 192), F32)], "mix"
    )(kept, swap(sent, "core"))
    taken = swap(sent, "half")

    reduced = jnp.sum(arrived.astype(F32), axis=0).astype(BF16)
    reduced, both = lax.optimization_barrier((reduced, both))
    (copies,) = fuse(settle, [((32, 96, 128), BF16)], "settle")(reduced, swap_z(reduced, 2))
    qkv_grad, proj_grad = finish(exchange_pairs(copies))

    own_rows, block_out = fuse(back, [((128, 384), BF16), ((64, 192), BF16)], "back", flops=20 * 10**9)(
        both, taken, staying, skipped, held, ln_gain
    )
    (input_grad,) = fuse(unpermute, [((256, 384), BF16)], "unpermute")(
        own_rows, swap(own_rows, "core")
    )
    return (block_out, input_grad, qkv_grad, proj_grad)


def solution(mesh):
    grid = Mesh(
        np.asarray(mesh.devices).reshape(4, 4, 4, 2, 2), ("y", "z", "x", "half", "core")
    )
    placed = (
        P(TILE, None),
        P(),
        P(None, HEAD, None),
        P(None, HEAD),
        P(None, HEAD),
        P(None, HEAD),
        P(HEAD, None),
        P(HEAD, None),
        P(TILE, HEAD),
    )
    return jax.shard_map(
        local,
        mesh=grid,
        in_specs=placed,
        out_specs=(P(TILE, HEAD), P(TILE, None), P(None, HEAD, None), P(HEAD, None)),
        check_vma=False,
    )
```

```python
import numpy as np

import jax
import jax.numpy as jnp
from jax import lax
from jax.experimental import pallas as pl
from jax.experimental.pallas import tpu as pltpu
from jax.sharding import Mesh
from jax.sharding import PartitionSpec as P

HEAD_DIM = 96
EPSILON = 1e-06
F32 = jnp.float32
BF16 = jnp.bfloat16
TILE = ("y", "z", "x")
HEAD = ("half", "core")
PLANE = ("y", "x")


def shift(block, axis, step):
    return lax.ppermute(block, axis, [(i, (i + step) % 4) for i in range(4)])


def swap(block, axis):
    return lax.ppermute(block, axis, [(0, 1), (1, 0)])


def swap_z(block, bit):
    return lax.ppermute(block, "z", [(i, i ^ bit) for i in range(4)])


def exchange_pairs(blocks):
    groups = [
        [16 * y + 4 * z + x for y in range(4) for z in (first, first + 1) for x in range(4)]
        for first in (0, 2)
    ]
    return lax.all_to_all(blocks, TILE, 0, 0, tiled=True, axis_index_groups=groups)


def exchange(blocks, axes):
    return lax.all_to_all(blocks, axes, 0, 0, tiled=True)


def sum_four(parts):
    wide = [p.astype(F32) for p in parts]
    return (wide[0] + wide[2]) + (wide[1] + wide[3])


def fuse(function, outs, name, direct=False, flops=None):
    def call(*operands):
        count, stored = len(operands), len(outs)

        def kernel(*refs):
            sources, targets = refs[:count], refs[count : count + stored]
            if direct:
                held = refs[count + stored : -1]
                fetches = [
                    pltpu.make_async_copy(source, target, refs[-1].at[i])
                    for i, (source, target) in enumerate(zip(sources, held))
                ]
                for fetch in fetches:
                    fetch.start()
                for fetch in fetches:
                    fetch.wait()
                sources = held
            results = function(*[ref[...] for ref in sources])
            for ref, result in zip(targets, results):
                ref[...] = result

        scratch = []
        if direct:
            scratch = [pltpu.VMEM(x.shape, x.dtype) for x in operands]
            scratch.append(pltpu.SemaphoreType.DMA((count,)))
        return pl.pallas_call(
            kernel,
            out_shape=[jax.ShapeDtypeStruct(shape, dtype) for shape, dtype in outs],
            in_specs=[pl.BlockSpec(memory_space=pl.ANY if direct else pltpu.VMEM)] * count,
            out_specs=[pl.BlockSpec(memory_space=pltpu.VMEM)] * stored,
            scratch_shapes=scratch,
            compiler_params=pltpu.CompilerParams(vmem_limit_bytes=(60 if direct else 32) * 1024 * 1024),
            cost_estimate=flops
            and pl.CostEstimate(flops=flops, bytes_accessed=0, transcendentals=0),
            name=name,
        )(*operands)

    return call


def either(which, first, second):
    return jnp.where(which == 0, first, second)


def dot(a, b, contract):
    return lax.dot_general(a, b, (contract, ((), ())), preferred_element_type=F32)


def dot_nn(a, b):
    return dot(a, b, ((1,), (0,)))


def dot_nt(a, b):
    return dot(a, b, ((1,), (1,)))


def dot_tn(a, b):
    return dot(a, b, ((0,), (0,)))


def token_of(place):
    a, b, r, c = place >> 6, (place >> 4) & 3, (place >> 3) & 1, place & 7
    return (4 * r + a) * 32 + 4 * c + b


def query_of(place):
    a, b, r, c = place >> 5, (place >> 4) & 1, (place >> 3) & 1, place & 7
    return (2 * r + a) * 16 + 2 * c + b


def selector(count, source, transposed):
    rows = lax.broadcasted_iota(jnp.int32, (count, count), 0)
    columns = lax.broadcasted_iota(jnp.int32, (count, count), 1)
    hit = source(columns) == rows if transposed else source(rows) == columns
    return jnp.where(hit, 1.0, 0.0).astype(BF16)


def normalize(values_in):
    center = values_in - jnp.mean(values_in, axis=-1, keepdims=True)
    inv_std = lax.rsqrt(jnp.mean(center * center, axis=-1, keepdims=True) + EPSILON)
    return center * inv_std, inv_std


def pool_keys(feature, weight):
    wide = weight.astype(F32)
    total = wide[0:1] * feature[0:16]
    for k in range(1, 16):
        total = total + wide[k : k + 1] * feature[16 * k : 16 * k + 16]
    return total


def spread_keys(upstream, weight):
    wide = weight.astype(F32)
    return jnp.concatenate([wide[k : k + 1] * upstream for k in range(16)], axis=0)


def query_blocks():
    out = []
    for a2 in range(2):
        for b2 in range(2):
            out.append(
                [
                    (2 * a1 + b1, (2 * a2 + a1) * 4 + 2 * b2 + b1)
                    for a1 in range(2)
                    for b1 in range(2)
                ]
            )
    return out


def pool_queries(feature, weight):
    wide = weight.astype(F32)
    rows = []
    for members in query_blocks():
        total = None
        for tap, block in members:
            term = feature[16 * block : 16 * block + 16]
            if weight is not None:
                term = wide[tap : tap + 1] * term
            total = term if total is None else total + term
        rows.append(total)
    return jnp.concatenate(rows, axis=0)


def spread_queries(upstream, weight):
    wide = weight.astype(F32)
    blocks = [None] * 16
    for place, members in enumerate(query_blocks()):
        for tap, block in members:
            blocks[block] = wide[tap : tap + 1] * upstream[16 * place : 16 * place + 16]
    return jnp.concatenate(blocks, axis=0)


def front(tokens, ln_gain, weight_kv, key_pool, value_pool):
    held = dot_nn(selector(256, token_of, False), tokens)
    unit, _ = normalize(held)
    normed = (unit * ln_gain[None, :]).astype(BF16)
    key_pooled = pool_keys(dot_nt(normed, weight_kv[1]), key_pool)
    value_pooled = pool_keys(dot_nt(normed, weight_kv[2]), value_pool)
    blank = jnp.zeros((16, 64), F32)
    rows = [
        jnp.concatenate([key_pooled[:, part], value_pooled[:, part], blank], axis=1)
        for part in (slice(0, HEAD_DIM), slice(HEAD_DIM, 2 * HEAD_DIM))
    ]
    rows = jnp.concatenate(rows, axis=0).astype(BF16)
    return rows, rows, normed, held.astype(BF16)


def fold_rows(rows_in):
    count = rows_in.shape[0] // 2
    return jnp.concatenate([rows_in[:count, :192], rows_in[count:, :192]], axis=1)


def unfold_rows(rows_in):
    return jnp.concatenate([rows_in[:, :192], rows_in[:, 192:]], axis=0)


def copy_pair(own, other):
    wide, other = own.astype(F32), other.astype(F32)
    heads = [
        fold_rows(jnp.concatenate([wide[start : start + 16], other[start : start + 16]], axis=0))
        for start in (0, 16)
    ]
    heads = jnp.concatenate([jnp.broadcast_to(h[None, None], (1, 4, 16, 384)) for h in heads])
    return (jnp.broadcast_to(heads[None], (4, 2, 4, 16, 384)).astype(BF16).reshape(32, 16, 384),)


def middle(
    normed, held, weight_q, query_pool, cot_0, cot_1, cot_2, cot_3, proj_weight, skip_weight
):
    core, half = lax.axis_index("core"), lax.axis_index("half")
    pairs = [
        jnp.concatenate([either(core, p, q), either(core, q, p)], axis=1)
        for p, q in ((cot_0.astype(F32), cot_1.astype(F32)), (cot_2.astype(F32), cot_3.astype(F32)))
    ]
    full_cotangent = jnp.concatenate(
        [either(half, pairs[0], pairs[1]), either(half, pairs[1], pairs[0])], axis=1
    ).astype(BF16)
    query_pooled = pool_queries(dot_nt(normed, weight_q[0]), query_pool).astype(BF16)
    to_held = selector(64, query_of, False)
    held_cotangent = dot_nn(to_held, full_cotangent).astype(BF16)
    d_attended = dot_nt(held_cotangent, proj_weight).astype(BF16)
    ones = jnp.ones((4, held.shape[1]), F32)
    pooled_input = (pool_queries(held.astype(F32), ones) * 0.25).astype(BF16)
    natural = dot_nn(selector(64, query_of, True), pooled_input).astype(BF16)
    skipped = dot_nt(natural, skip_weight)
    own_cotangent = dot_nn(to_held, cot_0).astype(BF16)
    d_pooled = dot_nn(own_cotangent, skip_weight).astype(BF16)
    blank = jnp.zeros((64, 64), F32)
    queries, grads = query_pooled.astype(F32), d_attended.astype(F32)
    rows = [
        jnp.concatenate([queries[:, part], grads[:, part], blank], axis=1)
        for part in (slice(0, HEAD_DIM), slice(HEAD_DIM, 2 * HEAD_DIM))
    ]
    odd = lax.rem(lax.axis_index("z"), 2)
    mine = either(odd, rows[0], rows[1]).astype(BF16)
    theirs = either(odd, rows[1], rows[0]).astype(BF16)
    return mine, theirs, held_cotangent, skipped, d_pooled


def attend(rows_kv, mine, received):
    rows_kv = unfold_rows(rows_kv.reshape(512, 384))
    scale = HEAD_DIM ** (-0.5)
    wide = jnp.concatenate([mine, received], axis=0).astype(F32)[:, :192]
    lanes = lax.broadcasted_iota(jnp.int32, (128, 192), 1)
    on_keys = lanes < HEAD_DIM
    packed = jnp.concatenate(
        [jnp.where(on_keys, wide, 0.0), jnp.where(on_keys, 0.0, wide)], axis=0
    ).astype(BF16)
    products = dot_nt(packed, rows_kv)
    exp_scores = jnp.exp(products[:128] * scale)
    row_total = jnp.sum(exp_scores, axis=-1, keepdims=True)
    attn_probs = (exp_scores / row_total).astype(BF16)
    dprobs = products[128:]
    probs_wide = attn_probs.astype(F32)
    row_delta = jnp.sum(probs_wide * dprobs, axis=-1, keepdims=True)
    d_scores = (scale * probs_wide * (dprobs - row_delta)).astype(BF16)
    both = jnp.concatenate([d_scores, attn_probs], axis=0)
    rows_grad = fold_rows(dot_tn(both, packed)).astype(BF16).reshape(32, 16, 384)
    mixed = dot_nn(both, rows_kv)
    mixed = jnp.where(on_keys, mixed[:128], mixed[128:])
    mixed = mixed + jnp.concatenate([wide[:, HEAD_DIM:], wide[:, :HEAD_DIM]], axis=1)
    mixed = jnp.concatenate([mixed, jnp.zeros((128, 64), F32)], axis=1)
    return rows_grad, mixed[:64], mixed[64:].astype(BF16)


def cut(rows_in):
    return [rows_in[:, i : i + 128] for i in range(0, rows_in.shape[1], 128)]


def after(mixed, returned, normed, query_pool, held_cotangent, proj_weight):
    odd = lax.rem(lax.axis_index("z"), 2)
    returned = returned.astype(F32)
    first, second = either(odd, mixed, returned), either(odd, returned, mixed)
    query_grad = jnp.concatenate([first[:, :HEAD_DIM], second[:, :HEAD_DIM]], axis=1)
    attended = jnp.concatenate(
        [first[:, HEAD_DIM : 2 * HEAD_DIM], second[:, HEAD_DIM : 2 * HEAD_DIM]], axis=1
    ).astype(BF16)
    d_queries = spread_queries(query_grad, query_pool).astype(BF16)
    pieces = cut(dot_tn(d_queries, normed)) + cut(dot_tn(attended, held_cotangent))
    natural = dot_nn(selector(64, query_of, True), attended).astype(BF16)
    head_part = dot_nn(natural, proj_weight).astype(BF16)
    return jnp.stack(pieces).astype(BF16), d_queries, head_part


def tile_grads(own, other, key_pool, value_pool):
    total = own.astype(F32) + other.astype(F32)
    per_head = [total[:16], total[16:]]
    key_grad = jnp.concatenate([t[:, :HEAD_DIM] for t in per_head], axis=1)
    value_grad = jnp.concatenate([t[:, HEAD_DIM : 2 * HEAD_DIM] for t in per_head], axis=1)
    d_keys = spread_keys(key_grad, key_pool).astype(BF16)
    d_values = spread_keys(value_grad, value_pool).astype(BF16)
    return d_keys, d_values


def weights(own, other, normed, key_pool, value_pool, pieces):
    d_keys, d_values = tile_grads(own, other, key_pool, value_pool)
    more = jnp.stack(cut(dot_tn(d_keys, normed)) + cut(dot_tn(d_values, normed))).astype(BF16)
    blank = jnp.zeros((1, 192, 128), BF16)
    pieces = jnp.concatenate([pieces, more, blank], axis=0).reshape(32, 96, 128)
    return pieces, d_keys, d_values


def spread(d_keys, d_values, d_queries, qkv_weight, d_pooled, head_part, held, ln_gain):
    core = lax.axis_index("core")
    d_normed = dot_nn(d_queries, qkv_weight[0])
    d_normed = d_normed + dot_nn(d_keys, qkv_weight[1])
    d_normed = d_normed + dot_nn(d_values, qkv_weight[2])
    unit, inv_std = normalize(held.astype(F32))
    scaled = d_normed * ln_gain[None, :]
    grad = inv_std * (
        scaled
        - jnp.mean(scaled, axis=-1, keepdims=True)
        - unit * jnp.mean(scaled * unit, axis=-1, keepdims=True)
    )
    pooled, rows = d_pooled.astype(F32) * 0.25, head_part.astype(F32)
    grown = []
    for block in range(16):
        place = 2 * (block // 8) + (block % 4) // 2
        grown.append(pooled[16 * place : 16 * place + 16])
    grad = (grad + jnp.concatenate(grown, axis=0)).astype(BF16)
    grad = dot_nn(selector(256, token_of, True), grad)
    loads = []
    for c in range(2):
        channels = [rows[:, 192 * (2 * p + c) : 192 * (2 * p + c) + 192] for p in range(2)]
        loads.append(
            jnp.concatenate(
                [
                    grad[128 * c : 128 * c + 128],
                    jnp.concatenate(channels, axis=1),
                ],
                axis=0,
            )
        )
    kept = either(core, loads[0], loads[1]).astype(BF16)
    sent = either(core, loads[1], loads[0]).astype(BF16)
    return kept, sent


def settle(part_0, part_1):
    total = (part_0.astype(F32) + part_1.astype(F32)).astype(BF16)
    return (jnp.broadcast_to(total[None], (32, *total.shape)),)


def pair_sum(arrived):
    arrived = arrived.reshape(4, 2, 4, 16, 384)
    own, other = [], []
    blank = jnp.zeros((16, 64), F32)
    for h in range(2):
        total = None
        for y in range(4):
            for x in range(4):
                block = arrived[y, h, x].astype(F32)
                total = block if total is None else total + block
        own.append(jnp.concatenate([total[:, :192], blank], axis=1))
        other.append(jnp.concatenate([total[:, 192:], blank], axis=1))
    return jnp.concatenate(own, axis=0).astype(BF16), jnp.concatenate(other, axis=0).astype(BF16)


def finish(pieces):
    parts = [(0, 0), (1, 3), (1, 6), (0, 9), (0, 12)]

    def kernel(source, qkv_grad, proj_grad, room, semaphores):
        copies = []
        for i, (output, start) in enumerate(parts):
            for lane in range(3):
                piece = source[2 * (start + lane) : 2 * (start + lane) + 2].reshape(192, 128)
                room[i, :, 128 * lane : 128 * lane + 128] = piece.astype(F32)
            if output == 0:
                target = qkv_grad.at[(0, None, None, 1, 2)[i]]
            else:
                target = proj_grad.at[:, pl.ds(384 * (i - 1), 384)]
            copies.append(pltpu.make_async_copy(room.at[i], target, semaphores.at[i]))
            copies[-1].start()
        for copy in copies:
            copy.wait()

    return pl.pallas_call(
        kernel,
        out_shape=[
            jax.ShapeDtypeStruct((3, 192, 384), F32),
            jax.ShapeDtypeStruct((192, 768), F32),
        ],
        in_specs=[pl.BlockSpec(memory_space=pltpu.VMEM)],
        out_specs=[pl.BlockSpec(memory_space=pl.ANY)] * 2,
        scratch_shapes=[pltpu.VMEM((5, 192, 384), F32), pltpu.SemaphoreType.DMA((5,))],
        compiler_params=pltpu.CompilerParams(vmem_limit_bytes=32 * 1024 * 1024),
        name="finish",
    )(pieces)


def mix(kept, received):
    half = lax.axis_index("half")
    both = kept.astype(F32) + received.astype(F32)
    rows = [both[128:, :192], both[128:, 192:]]
    leaving = either(half, rows[1], rows[0])
    staying = either(half, rows[0], rows[1])
    folded = jnp.concatenate([leaving[:32], leaving[32:]], axis=1)
    sent = jnp.concatenate([both[:128], folded], axis=0).astype(BF16)
    return both[:128].astype(BF16), sent, staying


def back(both, taken, staying, skipped):
    rows = both.astype(F32) + taken[:128].astype(F32)
    folded = taken[128:].astype(F32)
    arrived = jnp.concatenate([folded[:, :192], folded[:, 192:]], axis=0)
    return rows.astype(BF16), (staying + arrived + skipped).astype(BF16)


def join(own_rows, other_rows):
    core = lax.axis_index("core")
    own_rows, other_rows = own_rows.astype(F32), other_rows.astype(F32)
    rows = [either(core, own_rows, other_rows), either(core, other_rows, own_rows)]
    return (jnp.concatenate(rows, axis=0).astype(BF16),)


def local(
    tokens,
    ln_gain,
    qkv_weight,
    query_pool,
    key_pool,
    value_pool,
    proj_weight,
    skip_weight,
    cotangent,
):
    cot_near = swap(cotangent, "core")

    own_kv, sent_kv, normed, held = fuse(
        front,
        [((32, 256), BF16)] * 2 + [((256, 384), BF16)] * 2,
        "front",
        direct=True,
    )(tokens, ln_gain, qkv_weight, key_pool, value_pool)
    other_kv = swap_z(sent_kv, 2)
    leaving, held = lax.optimization_barrier((cotangent, held))
    cot_far = swap(leaving, "half")
    (copies_kv,) = fuse(copy_pair, [((32, 16, 384), BF16)], "copy_pair")(own_kv, other_kv)
    copies_kv, cot_far, cot_near = lax.optimization_barrier((copies_kv, cot_far, cot_near))
    cot_both = swap(cot_far, "core")
    rows_kv = exchange_pairs(copies_kv)

    mine, theirs, held_cotangent, skipped, d_pooled = fuse(
        middle,
        [
            ((64, 256), BF16),
            ((64, 256), BF16),
            ((64, 768), BF16),
            ((64, 192), F32),
            ((64, 384), BF16),
        ],
        "middle",
    )(
        normed,
        held,
        qkv_weight,
        query_pool,
        cotangent,
        cot_near,
        cot_far,
        cot_both,
        proj_weight,
        skip_weight,
    )
    rows_grad, mixed, returned = fuse(
        attend, [((32, 16, 384), BF16), ((64, 256), F32), ((64, 256), BF16)], "attend"
    )(rows_kv, mine, swap_z(theirs, 1))

    arrived = exchange_pairs(rows_grad)
    own_grad, other_grad = fuse(pair_sum, [((32, 256), BF16)] * 2, "pair_sum")(arrived)
    other_grad = swap_z(other_grad, 2)
    pieces, d_queries, head_part = fuse(
        after, [((9, 192, 128), BF16), ((256, 192), BF16), ((64, 768), BF16)], "after"
    )(mixed, swap_z(returned, 1), normed, query_pool, held_cotangent, proj_weight)

    pieces, d_keys, d_values = fuse(
        weights, [((32, 96, 128), BF16)] + [((256, 192), BF16)] * 2, "weights"
    )(own_grad, other_grad, normed, key_pool, value_pool, pieces)
    arrived = exchange_pairs(pieces)
    kept, sent = fuse(spread, [((192, 384), BF16)] * 2, "spread")(
        d_keys, d_values, d_queries, qkv_weight, d_pooled, head_part, held, ln_gain
    )

    both, sent, staying = fuse(
        mix, [((128, 384), BF16), ((160, 384), BF16), ((64, 192), F32)], "mix"
    )(kept, swap(sent, "core"))
    taken = swap(sent, "half")

    reduced = jnp.sum(arrived.astype(F32), axis=0).astype(BF16)
    reduced, both = lax.optimization_barrier((reduced, both))
    (copies,) = fuse(settle, [((32, 96, 128), BF16)], "settle")(reduced, swap_z(reduced, 2))
    qkv_grad, proj_grad = finish(exchange_pairs(copies))

    own_rows, block_out = fuse(back, [((128, 384), BF16), ((64, 192), BF16)], "back", flops=20 * 10**9)(
        both, taken, staying, skipped
    )
    (input_grad,) = fuse(join, [((256, 384), BF16)], "join")(
        own_rows, swap(own_rows, "core")
    )
    return (block_out, input_grad, qkv_grad, proj_grad)


def solution(mesh):
    grid = Mesh(
        np.asarray(mesh.devices).reshape(4, 4, 4, 2, 2), ("y", "z", "x", "half", "core")
    )
    placed = (
        P(TILE, None),
        P(),
        P(None, HEAD, None),
        P(None, HEAD),
        P(None, HEAD),
        P(None, HEAD),
        P(HEAD, None),
        P(HEAD, None),
        P(TILE, HEAD),
    )
    return jax.shard_map(
        local,
        mesh=grid,
        in_specs=placed,
        out_specs=(P(TILE, HEAD), P(TILE, None), P(None, HEAD, None), P(HEAD, None)),
        check_vma=False,
    )
```

```python
import numpy as np

import jax
import jax.numpy as jnp
from jax import lax
from jax.experimental import pallas as pl
from jax.experimental.pallas import tpu as pltpu
from jax.sharding import Mesh
from jax.sharding import PartitionSpec as P

HEAD_DIM = 96
EPSILON = 1e-06
F32 = jnp.float32
BF16 = jnp.bfloat16
TILE = ("y", "z", "x")
HEAD = ("half", "core")
PLANE = ("y", "x")


def shift(block, axis, step):
    return lax.ppermute(block, axis, [(i, (i + step) % 4) for i in range(4)])


def swap(block, axis):
    return lax.ppermute(block, axis, [(0, 1), (1, 0)])


def swap_z(block, bit):
    return lax.ppermute(block, "z", [(i, i ^ bit) for i in range(4)])


def exchange_pairs(blocks):
    groups = [
        [16 * y + 4 * z + x for y in range(4) for z in (first, first + 1) for x in range(4)]
        for first in (0, 2)
    ]
    return lax.all_to_all(blocks, TILE, 0, 0, tiled=True, axis_index_groups=groups)


def exchange(blocks, axes):
    return lax.all_to_all(blocks, axes, 0, 0, tiled=True)


def sum_four(parts):
    wide = [p.astype(F32) for p in parts]
    return (wide[0] + wide[2]) + (wide[1] + wide[3])


def fuse(function, outs, name, direct=False, flops=None):
    def call(*operands):
        count, stored = len(operands), len(outs)

        def kernel(*refs):
            sources, targets = refs[:count], refs[count : count + stored]
            if direct:
                held = refs[count + stored : -1]
                fetches = [
                    pltpu.make_async_copy(source, target, refs[-1].at[i])
                    for i, (source, target) in enumerate(zip(sources, held))
                ]
                for fetch in fetches:
                    fetch.start()
                for fetch in fetches:
                    fetch.wait()
                sources = held
            results = function(*[ref[...] for ref in sources])
            for ref, result in zip(targets, results):
                ref[...] = result

        scratch = []
        if direct:
            scratch = [pltpu.VMEM(x.shape, x.dtype) for x in operands]
            scratch.append(pltpu.SemaphoreType.DMA((count,)))
        return pl.pallas_call(
            kernel,
            out_shape=[jax.ShapeDtypeStruct(shape, dtype) for shape, dtype in outs],
            in_specs=[pl.BlockSpec(memory_space=pl.ANY if direct else pltpu.VMEM)] * count,
            out_specs=[pl.BlockSpec(memory_space=pltpu.VMEM)] * stored,
            scratch_shapes=scratch,
            compiler_params=pltpu.CompilerParams(vmem_limit_bytes=(60 if direct else 32) * 1024 * 1024),
            cost_estimate=flops
            and pl.CostEstimate(flops=flops, bytes_accessed=0, transcendentals=0),
            name=name,
        )(*operands)

    return call


def either(which, first, second):
    return jnp.where(which == 0, first, second)


def dot(a, b, contract):
    return lax.dot_general(a, b, (contract, ((), ())), preferred_element_type=F32)


def dot_nn(a, b):
    return dot(a, b, ((1,), (0,)))


def dot_nt(a, b):
    return dot(a, b, ((1,), (1,)))


def dot_tn(a, b):
    return dot(a, b, ((0,), (0,)))


def token_of(place):
    a, b, r, c = place >> 6, (place >> 4) & 3, (place >> 3) & 1, place & 7
    return (4 * r + a) * 32 + 4 * c + b


def query_of(place):
    a, b, r, c = place >> 5, (place >> 4) & 1, (place >> 3) & 1, place & 7
    return (2 * r + a) * 16 + 2 * c + b


def selector(count, source, transposed):
    rows = lax.broadcasted_iota(jnp.int32, (count, count), 0)
    columns = lax.broadcasted_iota(jnp.int32, (count, count), 1)
    hit = source(columns) == rows if transposed else source(rows) == columns
    return jnp.where(hit, 1.0, 0.0).astype(BF16)


def normalize(values_in):
    center = values_in - jnp.mean(values_in, axis=-1, keepdims=True)
    inv_std = lax.rsqrt(jnp.mean(center * center, axis=-1, keepdims=True) + EPSILON)
    return center * inv_std, inv_std


def pool_keys(feature, weight):
    wide = weight.astype(F32)
    total = wide[0:1] * feature[0:16]
    for k in range(1, 16):
        total = total + wide[k : k + 1] * feature[16 * k : 16 * k + 16]
    return total


def spread_keys(upstream, weight):
    wide = weight.astype(F32)
    return jnp.concatenate([wide[k : k + 1] * upstream for k in range(16)], axis=0)


def query_blocks():
    out = []
    for a2 in range(2):
        for b2 in range(2):
            out.append(
                [
                    (2 * a1 + b1, (2 * a2 + a1) * 4 + 2 * b2 + b1)
                    for a1 in range(2)
                    for b1 in range(2)
                ]
            )
    return out


def pool_queries(feature, weight):
    wide = weight.astype(F32)
    rows = []
    for members in query_blocks():
        total = None
        for tap, block in members:
            term = feature[16 * block : 16 * block + 16]
            if weight is not None:
                term = wide[tap : tap + 1] * term
            total = term if total is None else total + term
        rows.append(total)
    return jnp.concatenate(rows, axis=0)


def spread_queries(upstream, weight):
    wide = weight.astype(F32)
    blocks = [None] * 16
    for place, members in enumerate(query_blocks()):
        for tap, block in members:
            blocks[block] = wide[tap : tap + 1] * upstream[16 * place : 16 * place + 16]
    return jnp.concatenate(blocks, axis=0)


def front(tokens, ln_gain, weight_kv, key_pool, value_pool):
    held = dot_nn(selector(256, token_of, False), tokens)
    unit, _ = normalize(held)
    normed = (unit * ln_gain[None, :]).astype(BF16)
    key_pooled = pool_keys(dot_nt(normed, weight_kv[1]), key_pool)
    value_pooled = pool_keys(dot_nt(normed, weight_kv[2]), value_pool)
    blank = jnp.zeros((16, 64), F32)
    rows = [
        jnp.concatenate([key_pooled[:, part], value_pooled[:, part], blank], axis=1)
        for part in (slice(0, HEAD_DIM), slice(HEAD_DIM, 2 * HEAD_DIM))
    ]
    rows = jnp.concatenate(rows, axis=0).astype(BF16)
    return rows, rows, normed, held.astype(BF16)


def fold_rows(rows_in):
    count = rows_in.shape[0] // 2
    return jnp.concatenate([rows_in[:count, :192], rows_in[count:, :192]], axis=1)


def unfold_rows(rows_in):
    return jnp.concatenate([rows_in[:, :192], rows_in[:, 192:]], axis=0)


def copy_pair(own, other):
    wide, other = own.astype(F32), other.astype(F32)
    heads = [
        fold_rows(jnp.concatenate([wide[start : start + 16], other[start : start + 16]], axis=0))
        for start in (0, 16)
    ]
    heads = jnp.concatenate([jnp.broadcast_to(h[None, None], (1, 4, 16, 384)) for h in heads])
    return (jnp.broadcast_to(heads[None], (4, 2, 4, 16, 384)).astype(BF16).reshape(32, 16, 384),)


def middle(
    normed, held, weight_q, query_pool, cot_0, cot_1, cot_2, cot_3, proj_weight, skip_weight
):
    core, half = lax.axis_index("core"), lax.axis_index("half")
    pairs = [
        jnp.concatenate([either(core, p, q), either(core, q, p)], axis=1)
        for p, q in ((cot_0.astype(F32), cot_1.astype(F32)), (cot_2.astype(F32), cot_3.astype(F32)))
    ]
    full_cotangent = jnp.concatenate(
        [either(half, pairs[0], pairs[1]), either(half, pairs[1], pairs[0])], axis=1
    ).astype(BF16)
    query_pooled = pool_queries(dot_nt(normed, weight_q[0]), query_pool).astype(BF16)
    to_held = selector(64, query_of, False)
    held_cotangent = dot_nn(to_held, full_cotangent).astype(BF16)
    d_attended = dot_nt(held_cotangent, proj_weight).astype(BF16)
    ones = jnp.ones((4, held.shape[1]), F32)
    pooled_input = (pool_queries(held.astype(F32), ones) * 0.25).astype(BF16)
    natural = dot_nn(selector(64, query_of, True), pooled_input).astype(BF16)
    skipped = dot_nt(natural, skip_weight)
    own_cotangent = dot_nn(to_held, cot_0).astype(BF16)
    d_pooled = dot_nn(own_cotangent, skip_weight).astype(BF16)
    blank = jnp.zeros((64, 64), F32)
    queries, grads = query_pooled.astype(F32), d_attended.astype(F32)
    rows = [
        jnp.concatenate([queries[:, part], grads[:, part], blank], axis=1)
        for part in (slice(0, HEAD_DIM), slice(HEAD_DIM, 2 * HEAD_DIM))
    ]
    odd = lax.rem(lax.axis_index("z"), 2)
    mine = either(odd, rows[0], rows[1]).astype(BF16)
    theirs = either(odd, rows[1], rows[0]).astype(BF16)
    return mine, theirs, held_cotangent, skipped, d_pooled


def attend(rows_kv, mine, received):
    rows_kv = unfold_rows(rows_kv.reshape(512, 384))
    scale = HEAD_DIM ** (-0.5)
    wide = jnp.concatenate([mine, received], axis=0).astype(F32)[:, :192]
    lanes = lax.broadcasted_iota(jnp.int32, (128, 192), 1)
    on_keys = lanes < HEAD_DIM
    packed = jnp.concatenate(
        [jnp.where(on_keys, wide, 0.0), jnp.where(on_keys, 0.0, wide)], axis=0
    ).astype(BF16)
    products = dot_nt(packed, rows_kv)
    exp_scores = jnp.exp(products[:128] * scale)
    row_total = jnp.sum(exp_scores, axis=-1, keepdims=True)
    attn_probs = (exp_scores / row_total).astype(BF16)
    dprobs = products[128:]
    probs_wide = attn_probs.astype(F32)
    row_delta = jnp.sum(probs_wide * dprobs, axis=-1, keepdims=True)
    d_scores = (scale * probs_wide * (dprobs - row_delta)).astype(BF16)
    both = jnp.concatenate([d_scores, attn_probs], axis=0)
    rows_grad = fold_rows(dot_tn(both, packed)).astype(BF16).reshape(32, 16, 384)
    mixed = dot_nn(both, rows_kv)
    mixed = jnp.where(on_keys, mixed[:128], mixed[128:])
    mixed = mixed + jnp.concatenate([wide[:, HEAD_DIM:], wide[:, :HEAD_DIM]], axis=1)
    mixed = jnp.concatenate([mixed, jnp.zeros((128, 64), F32)], axis=1)
    return rows_grad, mixed[:64], mixed[64:].astype(BF16)


def cut(rows_in):
    return [rows_in[:, i : i + 128] for i in range(0, rows_in.shape[1], 128)]


def after(mixed, returned, normed, query_pool, held_cotangent, proj_weight):
    odd = lax.rem(lax.axis_index("z"), 2)
    returned = returned.astype(F32)
    first, second = either(odd, mixed, returned), either(odd, returned, mixed)
    query_grad = jnp.concatenate([first[:, :HEAD_DIM], second[:, :HEAD_DIM]], axis=1)
    attended = jnp.concatenate(
        [first[:, HEAD_DIM : 2 * HEAD_DIM], second[:, HEAD_DIM : 2 * HEAD_DIM]], axis=1
    ).astype(BF16)
    d_queries = spread_queries(query_grad, query_pool).astype(BF16)
    pieces = cut(dot_tn(d_queries, normed)) + cut(dot_tn(attended, held_cotangent))
    natural = dot_nn(selector(64, query_of, True), attended).astype(BF16)
    head_part = dot_nn(natural, proj_weight).astype(BF16)
    return jnp.stack(pieces).astype(BF16).reshape(18, 96, 128), d_queries, head_part


def tile_grads(own, other, key_pool, value_pool):
    total = own.astype(F32) + other.astype(F32)
    per_head = [total[:16], total[16:]]
    key_grad = jnp.concatenate([t[:, :HEAD_DIM] for t in per_head], axis=1)
    value_grad = jnp.concatenate([t[:, HEAD_DIM : 2 * HEAD_DIM] for t in per_head], axis=1)
    d_keys = spread_keys(key_grad, key_pool).astype(BF16)
    d_values = spread_keys(value_grad, value_pool).astype(BF16)
    return d_keys, d_values


def weights(own_grad, other_grad, normed, key_pool, value_pool, pieces):
    def kernel(own, other, held, key_taps, value_taps, ready, out, d_keys, d_values, room, semaphores):
        first = pltpu.make_async_copy(ready, out.at[pl.ds(0, 18)], semaphores.at[0])
        first.start()
        d_keys[...], d_values[...] = tile_grads(
            own[...], other[...], key_taps[...], value_taps[...]
        )
        more = cut(dot_tn(d_keys[...], held[...])) + cut(dot_tn(d_values[...], held[...]))
        for i, piece in enumerate(more):
            room[2 * i] = piece[:96].astype(BF16)
            room[2 * i + 1] = piece[96:].astype(BF16)
        room[12] = jnp.zeros((96, 128), BF16)
        room[13] = jnp.zeros((96, 128), BF16)
        second = pltpu.make_async_copy(room, out.at[pl.ds(18, 14)], semaphores.at[1])
        second.start()
        first.wait()
        second.wait()

    vmem = pl.BlockSpec(memory_space=pltpu.VMEM)
    return pl.pallas_call(
        kernel,
        out_shape=[
            jax.ShapeDtypeStruct((32, 96, 128), BF16),
            jax.ShapeDtypeStruct((256, 192), BF16),
            jax.ShapeDtypeStruct((256, 192), BF16),
        ],
        in_specs=[vmem] * 6,
        out_specs=[pl.BlockSpec(memory_space=pl.ANY), vmem, vmem],
        scratch_shapes=[pltpu.VMEM((14, 96, 128), BF16), pltpu.SemaphoreType.DMA((2,))],
        compiler_params=pltpu.CompilerParams(vmem_limit_bytes=32 * 1024 * 1024),
        name="weights",
    )(own_grad, other_grad, normed, key_pool, value_pool, pieces)


def spread(d_keys, d_values, d_queries, qkv_weight, d_pooled, head_part, held, ln_gain):
    core = lax.axis_index("core")
    d_normed = dot_nn(d_queries, qkv_weight[0])
    d_normed = d_normed + dot_nn(d_keys, qkv_weight[1])
    d_normed = d_normed + dot_nn(d_values, qkv_weight[2])
    unit, inv_std = normalize(held.astype(F32))
    scaled = d_normed * ln_gain[None, :]
    grad = inv_std * (
        scaled
        - jnp.mean(scaled, axis=-1, keepdims=True)
        - unit * jnp.mean(scaled * unit, axis=-1, keepdims=True)
    )
    pooled, rows = d_pooled.astype(F32) * 0.25, head_part.astype(F32)
    grown = []
    for block in range(16):
        place = 2 * (block // 8) + (block % 4) // 2
        grown.append(pooled[16 * place : 16 * place + 16])
    grad = (grad + jnp.concatenate(grown, axis=0)).astype(BF16)
    grad = dot_nn(selector(256, token_of, True), grad)
    loads = []
    for c in range(2):
        channels = [rows[:, 192 * (2 * p + c) : 192 * (2 * p + c) + 192] for p in range(2)]
        loads.append(
            jnp.concatenate(
                [
                    grad[128 * c : 128 * c + 128],
                    jnp.concatenate(channels, axis=1),
                ],
                axis=0,
            )
        )
    kept = either(core, loads[0], loads[1]).astype(BF16)
    sent = either(core, loads[1], loads[0]).astype(BF16)
    return kept, sent


def settle(part_0, part_1):
    total = (part_0.astype(F32) + part_1.astype(F32)).astype(BF16)
    return (jnp.broadcast_to(total[None], (32, *total.shape)),)


def pair_sum(arrived):
    arrived = arrived.reshape(4, 2, 4, 16, 384)
    own, other = [], []
    blank = jnp.zeros((16, 64), F32)
    for h in range(2):
        total = None
        for y in range(4):
            for x in range(4):
                block = arrived[y, h, x].astype(F32)
                total = block if total is None else total + block
        own.append(jnp.concatenate([total[:, :192], blank], axis=1))
        other.append(jnp.concatenate([total[:, 192:], blank], axis=1))
    return jnp.concatenate(own, axis=0).astype(BF16), jnp.concatenate(other, axis=0).astype(BF16)


def finish(pieces):
    parts = [(0, 0), (1, 3), (1, 6), (0, 9), (0, 12)]

    def kernel(source, qkv_grad, proj_grad, room, semaphores):
        copies = []
        for i, (output, start) in enumerate(parts):
            for lane in range(3):
                piece = source[2 * (start + lane) : 2 * (start + lane) + 2].reshape(192, 128)
                room[i, :, 128 * lane : 128 * lane + 128] = piece.astype(F32)
            if output == 0:
                target = qkv_grad.at[(0, None, None, 1, 2)[i]]
            else:
                target = proj_grad.at[:, pl.ds(384 * (i - 1), 384)]
            copies.append(pltpu.make_async_copy(room.at[i], target, semaphores.at[i]))
            copies[-1].start()
        for copy in copies:
            copy.wait()

    return pl.pallas_call(
        kernel,
        out_shape=[
            jax.ShapeDtypeStruct((3, 192, 384), F32),
            jax.ShapeDtypeStruct((192, 768), F32),
        ],
        in_specs=[pl.BlockSpec(memory_space=pltpu.VMEM)],
        out_specs=[pl.BlockSpec(memory_space=pl.ANY)] * 2,
        scratch_shapes=[pltpu.VMEM((5, 192, 384), F32), pltpu.SemaphoreType.DMA((5,))],
        compiler_params=pltpu.CompilerParams(vmem_limit_bytes=32 * 1024 * 1024),
        name="finish",
    )(pieces)


def mix(kept, received):
    half = lax.axis_index("half")
    both = kept.astype(F32) + received.astype(F32)
    rows = [both[128:, :192], both[128:, 192:]]
    leaving = either(half, rows[1], rows[0])
    staying = either(half, rows[0], rows[1])
    folded = jnp.concatenate([leaving[:32], leaving[32:]], axis=1)
    sent = jnp.concatenate([both[:128], folded], axis=0).astype(BF16)
    return both[:128].astype(BF16), sent, staying


def back(both, taken, staying, skipped):
    rows = both.astype(F32) + taken[:128].astype(F32)
    folded = taken[128:].astype(F32)
    arrived = jnp.concatenate([folded[:, :192], folded[:, 192:]], axis=0)
    return rows.astype(BF16), (staying + arrived + skipped).astype(BF16)


def join(own_rows, other_rows):
    core = lax.axis_index("core")
    own_rows, other_rows = own_rows.astype(F32), other_rows.astype(F32)
    rows = [either(core, own_rows, other_rows), either(core, other_rows, own_rows)]
    return (jnp.concatenate(rows, axis=0).astype(BF16),)


def local(
    tokens,
    ln_gain,
    qkv_weight,
    query_pool,
    key_pool,
    value_pool,
    proj_weight,
    skip_weight,
    cotangent,
):
    cot_near = swap(cotangent, "core")

    own_kv, sent_kv, normed, held = fuse(
        front,
        [((32, 256), BF16)] * 2 + [((256, 384), BF16)] * 2,
        "front",
        direct=True,
    )(tokens, ln_gain, qkv_weight, key_pool, value_pool)
    other_kv = swap_z(sent_kv, 2)
    leaving, held = lax.optimization_barrier((cotangent, held))
    cot_far = swap(leaving, "half")
    (copies_kv,) = fuse(copy_pair, [((32, 16, 384), BF16)], "copy_pair")(own_kv, other_kv)
    copies_kv, cot_far, cot_near = lax.optimization_barrier((copies_kv, cot_far, cot_near))
    cot_both = swap(cot_far, "core")
    rows_kv = exchange_pairs(copies_kv)

    mine, theirs, held_cotangent, skipped, d_pooled = fuse(
        middle,
        [
            ((64, 256), BF16),
            ((64, 256), BF16),
            ((64, 768), BF16),
            ((64, 192), F32),
            ((64, 384), BF16),
        ],
        "middle",
    )(
        normed,
        held,
        qkv_weight,
        query_pool,
        cotangent,
        cot_near,
        cot_far,
        cot_both,
        proj_weight,
        skip_weight,
    )
    rows_grad, mixed, returned = fuse(
        attend, [((32, 16, 384), BF16), ((64, 256), F32), ((64, 256), BF16)], "attend"
    )(rows_kv, mine, swap_z(theirs, 1))

    arrived = exchange_pairs(rows_grad)
    own_grad, other_grad = fuse(pair_sum, [((32, 256), BF16)] * 2, "pair_sum")(arrived)
    other_grad = swap_z(other_grad, 2)
    pieces, d_queries, head_part = fuse(
        after, [((18, 96, 128), BF16), ((256, 192), BF16), ((64, 768), BF16)], "after"
    )(mixed, swap_z(returned, 1), normed, query_pool, held_cotangent, proj_weight)

    pieces, d_keys, d_values = weights(
        own_grad, other_grad, normed, key_pool, value_pool, pieces
    )
    arrived = exchange_pairs(pieces)
    kept, sent = fuse(spread, [((192, 384), BF16)] * 2, "spread")(
        d_keys, d_values, d_queries, qkv_weight, d_pooled, head_part, held, ln_gain
    )

    both, sent, staying = fuse(
        mix, [((128, 384), BF16), ((160, 384), BF16), ((64, 192), F32)], "mix"
    )(kept, swap(sent, "core"))

    reduced = jnp.sum(arrived.astype(F32), axis=0).astype(BF16)
    other_sums = swap_z(reduced, 2)
    other_sums, both, sent = lax.optimization_barrier((other_sums, both, sent))
    taken = swap(sent, "half")
    (copies,) = fuse(settle, [((32, 96, 128), BF16)], "settle")(reduced, other_sums)
    qkv_grad, proj_grad = finish(exchange_pairs(copies))

    own_rows, block_out = fuse(back, [((128, 384), BF16), ((64, 192), BF16)], "back", flops=20 * 10**9)(
        both, taken, staying, skipped
    )
    (input_grad,) = fuse(join, [((256, 384), BF16)], "join")(
        own_rows, swap(own_rows, "core")
    )
    return (block_out, input_grad, qkv_grad, proj_grad)


def solution(mesh):
    grid = Mesh(
        np.asarray(mesh.devices).reshape(4, 4, 4, 2, 2), ("y", "z", "x", "half", "core")
    )
    placed = (
        P(TILE, None),
        P(),
        P(None, HEAD, None),
        P(None, HEAD),
        P(None, HEAD),
        P(None, HEAD),
        P(HEAD, None),
        P(HEAD, None),
        P(TILE, HEAD),
    )
    return jax.shard_map(
        local,
        mesh=grid,
        in_specs=placed,
        out_specs=(P(TILE, HEAD), P(TILE, None), P(None, HEAD, None), P(HEAD, None)),
        check_vma=False,
    )
```

```python
import numpy as np

import jax
import jax.numpy as jnp
from jax import lax
from jax.experimental import pallas as pl
from jax.experimental.pallas import tpu as pltpu
from jax.sharding import Mesh
from jax.sharding import PartitionSpec as P

HEAD_DIM = 96
EPSILON = 1e-06
F32 = jnp.float32
BF16 = jnp.bfloat16
TILE = ("y", "z", "x")
HEAD = ("half", "core")
PLANE = ("y", "x")


def shift(block, axis, step):
    return lax.ppermute(block, axis, [(i, (i + step) % 4) for i in range(4)])


def swap(block, axis):
    return lax.ppermute(block, axis, [(0, 1), (1, 0)])


def swap_z(block, bit):
    return lax.ppermute(block, "z", [(i, i ^ bit) for i in range(4)])


def exchange_pairs(blocks):
    groups = [
        [16 * y + 4 * z + x for y in range(4) for z in (first, first + 1) for x in range(4)]
        for first in (0, 2)
    ]
    return lax.all_to_all(blocks, TILE, 0, 0, tiled=True, axis_index_groups=groups)


def exchange(blocks, axes):
    return lax.all_to_all(blocks, axes, 0, 0, tiled=True)


def sum_four(parts):
    wide = [p.astype(F32) for p in parts]
    return (wide[0] + wide[2]) + (wide[1] + wide[3])


def fuse(function, outs, name, direct=False, flops=None):
    def call(*operands):
        count, stored = len(operands), len(outs)

        def kernel(*refs):
            sources, targets = refs[:count], refs[count : count + stored]
            if direct:
                held = refs[count + stored : -1]
                fetches = [
                    pltpu.make_async_copy(source, target, refs[-1].at[i])
                    for i, (source, target) in enumerate(zip(sources, held))
                ]
                for fetch in fetches:
                    fetch.start()
                for fetch in fetches:
                    fetch.wait()
                sources = held
            results = function(*[ref[...] for ref in sources])
            for ref, result in zip(targets, results):
                ref[...] = result

        scratch = []
        if direct:
            scratch = [pltpu.VMEM(x.shape, x.dtype) for x in operands]
            scratch.append(pltpu.SemaphoreType.DMA((count,)))
        return pl.pallas_call(
            kernel,
            out_shape=[jax.ShapeDtypeStruct(shape, dtype) for shape, dtype in outs],
            in_specs=[pl.BlockSpec(memory_space=pl.ANY if direct else pltpu.VMEM)] * count,
            out_specs=[pl.BlockSpec(memory_space=pltpu.VMEM)] * stored,
            scratch_shapes=scratch,
            compiler_params=pltpu.CompilerParams(vmem_limit_bytes=(60 if direct else 32) * 1024 * 1024),
            cost_estimate=flops
            and pl.CostEstimate(flops=flops, bytes_accessed=0, transcendentals=0),
            name=name,
        )(*operands)

    return call


def either(which, first, second):
    return jnp.where(which == 0, first, second)


def dot(a, b, contract):
    return lax.dot_general(a, b, (contract, ((), ())), preferred_element_type=F32)


def dot_nn(a, b):
    return dot(a, b, ((1,), (0,)))


def dot_nt(a, b):
    return dot(a, b, ((1,), (1,)))


def dot_tn(a, b):
    return dot(a, b, ((0,), (0,)))


def token_of(place):
    a, b, r, c = place >> 6, (place >> 4) & 3, (place >> 3) & 1, place & 7
    return (4 * r + a) * 32 + 4 * c + b


def query_of(place):
    a, b, r, c = place >> 5, (place >> 4) & 1, (place >> 3) & 1, place & 7
    return (2 * r + a) * 16 + 2 * c + b


def selector(count, source, transposed):
    rows = lax.broadcasted_iota(jnp.int32, (count, count), 0)
    columns = lax.broadcasted_iota(jnp.int32, (count, count), 1)
    hit = source(columns) == rows if transposed else source(rows) == columns
    return jnp.where(hit, 1.0, 0.0).astype(BF16)


def normalize(values_in):
    center = values_in - jnp.mean(values_in, axis=-1, keepdims=True)
    inv_std = lax.rsqrt(jnp.mean(center * center, axis=-1, keepdims=True) + EPSILON)
    return center * inv_std, inv_std


def pool_keys(feature, weight):
    wide = weight.astype(F32)
    total = wide[0:1] * feature[0:16]
    for k in range(1, 16):
        total = total + wide[k : k + 1] * feature[16 * k : 16 * k + 16]
    return total


def spread_keys(upstream, weight):
    wide = weight.astype(F32)
    return jnp.concatenate([wide[k : k + 1] * upstream for k in range(16)], axis=0)


def query_blocks():
    out = []
    for a2 in range(2):
        for b2 in range(2):
            out.append(
                [
                    (2 * a1 + b1, (2 * a2 + a1) * 4 + 2 * b2 + b1)
                    for a1 in range(2)
                    for b1 in range(2)
                ]
            )
    return out


def pool_queries(feature, weight):
    wide = weight.astype(F32)
    rows = []
    for members in query_blocks():
        total = None
        for tap, block in members:
            term = feature[16 * block : 16 * block + 16]
            if weight is not None:
                term = wide[tap : tap + 1] * term
            total = term if total is None else total + term
        rows.append(total)
    return jnp.concatenate(rows, axis=0)


def spread_queries(upstream, weight):
    wide = weight.astype(F32)
    blocks = [None] * 16
    for place, members in enumerate(query_blocks()):
        for tap, block in members:
            blocks[block] = wide[tap : tap + 1] * upstream[16 * place : 16 * place + 16]
    return jnp.concatenate(blocks, axis=0)


def front(tokens, ln_gain, weight_kv, key_pool, value_pool):
    held = dot_nn(selector(256, token_of, False), tokens)
    unit, _ = normalize(held)
    normed = (unit * ln_gain[None, :]).astype(BF16)
    key_pooled = pool_keys(dot_nt(normed, weight_kv[1]), key_pool)
    value_pooled = pool_keys(dot_nt(normed, weight_kv[2]), value_pool)
    blank = jnp.zeros((16, 64), F32)
    rows = [
        jnp.concatenate([key_pooled[:, part], value_pooled[:, part], blank], axis=1)
        for part in (slice(0, HEAD_DIM), slice(HEAD_DIM, 2 * HEAD_DIM))
    ]
    rows = jnp.concatenate(rows, axis=0).astype(BF16)
    return rows, rows, normed, held.astype(BF16)


def fold_rows(rows_in):
    count = rows_in.shape[0] // 2
    return jnp.concatenate([rows_in[:count, :192], rows_in[count:, :192]], axis=1)


def unfold_rows(rows_in):
    return jnp.concatenate([rows_in[:, :192], rows_in[:, 192:]], axis=0)


def copy_pair(own, other):
    wide, other = own.astype(F32), other.astype(F32)
    heads = [
        fold_rows(jnp.concatenate([wide[start : start + 16], other[start : start + 16]], axis=0))
        for start in (0, 16)
    ]
    heads = jnp.concatenate([jnp.broadcast_to(h[None, None], (1, 4, 16, 384)) for h in heads])
    return (jnp.broadcast_to(heads[None], (4, 2, 4, 16, 384)).astype(BF16).reshape(32, 16, 384),)


def middle(
    normed, held, weight_q, query_pool, cot_0, cot_1, cot_2, cot_3, proj_weight, skip_weight
):
    core, half = lax.axis_index("core"), lax.axis_index("half")
    pairs = [
        jnp.concatenate([either(core, p, q), either(core, q, p)], axis=1)
        for p, q in ((cot_0.astype(F32), cot_1.astype(F32)), (cot_2.astype(F32), cot_3.astype(F32)))
    ]
    full_cotangent = jnp.concatenate(
        [either(half, pairs[0], pairs[1]), either(half, pairs[1], pairs[0])], axis=1
    ).astype(BF16)
    query_pooled = pool_queries(dot_nt(normed, weight_q[0]), query_pool).astype(BF16)
    to_held = selector(64, query_of, False)
    held_cotangent = dot_nn(to_held, full_cotangent).astype(BF16)
    d_attended = dot_nt(held_cotangent, proj_weight).astype(BF16)
    ones = jnp.ones((4, held.shape[1]), F32)
    pooled_input = (pool_queries(held.astype(F32), ones) * 0.25).astype(BF16)
    natural = dot_nn(selector(64, query_of, True), pooled_input).astype(BF16)
    skipped = dot_nt(natural, skip_weight)
    own_cotangent = dot_nn(to_held, cot_0).astype(BF16)
    d_pooled = dot_nn(own_cotangent, skip_weight).astype(BF16)
    blank = jnp.zeros((64, 64), F32)
    queries, grads = query_pooled.astype(F32), d_attended.astype(F32)
    rows = [
        jnp.concatenate([queries[:, part], grads[:, part], blank], axis=1)
        for part in (slice(0, HEAD_DIM), slice(HEAD_DIM, 2 * HEAD_DIM))
    ]
    odd = lax.rem(lax.axis_index("z"), 2)
    mine = either(odd, rows[0], rows[1]).astype(BF16)
    theirs = either(odd, rows[1], rows[0]).astype(BF16)
    return mine, theirs, held_cotangent, skipped, d_pooled


def attend(rows_kv, mine, received):
    rows_kv = unfold_rows(rows_kv.reshape(512, 384))
    scale = HEAD_DIM ** (-0.5)
    wide = jnp.concatenate([mine, received], axis=0).astype(F32)[:, :192]
    lanes = lax.broadcasted_iota(jnp.int32, (128, 192), 1)
    on_keys = lanes < HEAD_DIM
    packed = jnp.concatenate(
        [jnp.where(on_keys, wide, 0.0), jnp.where(on_keys, 0.0, wide)], axis=0
    ).astype(BF16)
    products = dot_nt(packed, rows_kv)
    exp_scores = jnp.exp(products[:128] * scale)
    row_total = jnp.sum(exp_scores, axis=-1, keepdims=True)
    attn_probs = (exp_scores / row_total).astype(BF16)
    dprobs = products[128:]
    probs_wide = attn_probs.astype(F32)
    row_delta = jnp.sum(probs_wide * dprobs, axis=-1, keepdims=True)
    d_scores = (scale * probs_wide * (dprobs - row_delta)).astype(BF16)
    both = jnp.concatenate([d_scores, attn_probs], axis=0)
    rows_grad = fold_rows(dot_tn(both, packed)).astype(BF16).reshape(32, 16, 384)
    mixed = dot_nn(both, rows_kv)
    mixed = jnp.where(on_keys, mixed[:128], mixed[128:])
    mixed = mixed + jnp.concatenate([wide[:, HEAD_DIM:], wide[:, :HEAD_DIM]], axis=1)
    mixed = jnp.concatenate([mixed, jnp.zeros((128, 64), F32)], axis=1)
    return rows_grad, mixed[:64], mixed[64:].astype(BF16)


def cut(rows_in):
    return [rows_in[:, i : i + 128] for i in range(0, rows_in.shape[1], 128)]


def after(mixed, returned, normed, query_pool, held_cotangent, proj_weight):
    odd = lax.rem(lax.axis_index("z"), 2)
    returned = returned.astype(F32)
    first, second = either(odd, mixed, returned), either(odd, returned, mixed)
    query_grad = jnp.concatenate([first[:, :HEAD_DIM], second[:, :HEAD_DIM]], axis=1)
    attended = jnp.concatenate(
        [first[:, HEAD_DIM : 2 * HEAD_DIM], second[:, HEAD_DIM : 2 * HEAD_DIM]], axis=1
    ).astype(BF16)
    d_queries = spread_queries(query_grad, query_pool).astype(BF16)
    pieces = cut(dot_tn(d_queries, normed)) + cut(dot_tn(attended, held_cotangent))
    natural = dot_nn(selector(64, query_of, True), attended).astype(BF16)
    head_part = dot_nn(natural, proj_weight).astype(BF16)
    return jnp.stack(pieces).astype(BF16).reshape(18, 96, 128), d_queries, head_part


def tile_grads(own, other, key_pool, value_pool):
    total = own.astype(F32) + other.astype(F32)
    per_head = [total[:16], total[16:]]
    key_grad = jnp.concatenate([t[:, :HEAD_DIM] for t in per_head], axis=1)
    value_grad = jnp.concatenate([t[:, HEAD_DIM : 2 * HEAD_DIM] for t in per_head], axis=1)
    d_keys = spread_keys(key_grad, key_pool).astype(BF16)
    d_values = spread_keys(value_grad, value_pool).astype(BF16)
    return d_keys, d_values


def weights(own_grad, other_grad, normed, key_pool, value_pool, pieces):
    def kernel(own, other, held, key_taps, value_taps, ready, out, d_keys, d_values, room, semaphores):
        first = pltpu.make_async_copy(ready, out.at[pl.ds(0, 18)], semaphores.at[0])
        first.start()
        d_keys[...], d_values[...] = tile_grads(
            own[...], other[...], key_taps[...], value_taps[...]
        )
        more = cut(dot_tn(d_keys[...], held[...])) + cut(dot_tn(d_values[...], held[...]))
        for i, piece in enumerate(more):
            room[2 * i] = piece[:96].astype(BF16)
            room[2 * i + 1] = piece[96:].astype(BF16)
        room[12] = jnp.zeros((96, 128), BF16)
        room[13] = jnp.zeros((96, 128), BF16)
        second = pltpu.make_async_copy(room, out.at[pl.ds(18, 14)], semaphores.at[1])
        second.start()
        first.wait()
        second.wait()

    vmem = pl.BlockSpec(memory_space=pltpu.VMEM)
    return pl.pallas_call(
        kernel,
        out_shape=[
            jax.ShapeDtypeStruct((32, 96, 128), BF16),
            jax.ShapeDtypeStruct((256, 192), BF16),
            jax.ShapeDtypeStruct((256, 192), BF16),
        ],
        in_specs=[vmem] * 6,
        out_specs=[pl.BlockSpec(memory_space=pl.ANY), vmem, vmem],
        scratch_shapes=[pltpu.VMEM((14, 96, 128), BF16), pltpu.SemaphoreType.DMA((2,))],
        compiler_params=pltpu.CompilerParams(vmem_limit_bytes=32 * 1024 * 1024),
        name="weights",
    )(own_grad, other_grad, normed, key_pool, value_pool, pieces)


def spread(d_keys, d_values, d_queries, qkv_weight, d_pooled, head_part, held, ln_gain):
    core = lax.axis_index("core")
    d_normed = dot_nn(d_queries, qkv_weight[0])
    d_normed = d_normed + dot_nn(d_keys, qkv_weight[1])
    d_normed = d_normed + dot_nn(d_values, qkv_weight[2])
    unit, inv_std = normalize(held.astype(F32))
    scaled = d_normed * ln_gain[None, :]
    grad = inv_std * (
        scaled
        - jnp.mean(scaled, axis=-1, keepdims=True)
        - unit * jnp.mean(scaled * unit, axis=-1, keepdims=True)
    )
    pooled, rows = d_pooled.astype(F32) * 0.25, head_part.astype(F32)
    grown = []
    for block in range(16):
        place = 2 * (block // 8) + (block % 4) // 2
        grown.append(pooled[16 * place : 16 * place + 16])
    grad = (grad + jnp.concatenate(grown, axis=0)).astype(BF16)
    grad = dot_nn(selector(256, token_of, True), grad)
    loads = []
    for c in range(2):
        channels = [rows[:, 192 * (2 * p + c) : 192 * (2 * p + c) + 192] for p in range(2)]
        loads.append(
            jnp.concatenate(
                [
                    grad[128 * c : 128 * c + 128],
                    jnp.concatenate(channels, axis=1),
                ],
                axis=0,
            )
        )
    kept = either(core, loads[0], loads[1]).astype(BF16)
    sent = either(core, loads[1], loads[0]).astype(BF16)
    return kept, sent


def settle(part_0, part_1):
    total = (part_0.astype(F32) + part_1.astype(F32)).astype(BF16)
    return (jnp.broadcast_to(total[None], (32, *total.shape)),)


def pair_sum(arrived):
    arrived = arrived.reshape(4, 2, 4, 16, 384)
    own, other = [], []
    blank = jnp.zeros((16, 64), F32)
    for h in range(2):
        total = None
        for y in range(4):
            for x in range(4):
                block = arrived[y, h, x].astype(F32)
                total = block if total is None else total + block
        own.append(jnp.concatenate([total[:, :192], blank], axis=1))
        other.append(jnp.concatenate([total[:, 192:], blank], axis=1))
    return jnp.concatenate(own, axis=0).astype(BF16), jnp.concatenate(other, axis=0).astype(BF16)


def finish(pieces):
    parts = [(0, 0), (1, 3), (1, 6), (0, 9), (0, 12)]

    def kernel(source, qkv_grad, proj_grad, room, semaphores):
        copies = []
        for i, (output, start) in enumerate(parts):
            for lane in range(3):
                piece = source[2 * (start + lane) : 2 * (start + lane) + 2].reshape(192, 128)
                room[i, :, 128 * lane : 128 * lane + 128] = piece.astype(F32)
            if output == 0:
                target = qkv_grad.at[(0, None, None, 1, 2)[i]]
            else:
                target = proj_grad.at[:, pl.ds(384 * (i - 1), 384)]
            copies.append(pltpu.make_async_copy(room.at[i], target, semaphores.at[i]))
            copies[-1].start()
        for copy in copies:
            copy.wait()

    return pl.pallas_call(
        kernel,
        out_shape=[
            jax.ShapeDtypeStruct((3, 192, 384), F32),
            jax.ShapeDtypeStruct((192, 768), F32),
        ],
        in_specs=[pl.BlockSpec(memory_space=pltpu.VMEM)],
        out_specs=[pl.BlockSpec(memory_space=pl.ANY)] * 2,
        scratch_shapes=[pltpu.VMEM((5, 192, 384), F32), pltpu.SemaphoreType.DMA((5,))],
        compiler_params=pltpu.CompilerParams(vmem_limit_bytes=32 * 1024 * 1024),
        name="finish",
    )(pieces)


def mix(kept, received):
    half = lax.axis_index("half")
    both = kept.astype(F32) + received.astype(F32)
    rows = [both[128:, :192], both[128:, 192:]]
    leaving = either(half, rows[1], rows[0])
    staying = either(half, rows[0], rows[1])
    folded = jnp.concatenate([leaving[:32], leaving[32:]], axis=1)
    sent = jnp.concatenate([both[:128], folded], axis=0).astype(BF16)
    return both[:128].astype(BF16), sent, staying


def back(both, taken, staying, skipped):
    rows = both.astype(F32) + taken[:128].astype(F32)
    folded = taken[128:].astype(F32)
    arrived = jnp.concatenate([folded[:, :192], folded[:, 192:]], axis=0)
    return rows.astype(BF16), (staying + arrived + skipped).astype(BF16)


def join(own_rows, other_rows):
    core = lax.axis_index("core")
    own_rows, other_rows = own_rows.astype(F32), other_rows.astype(F32)
    rows = [either(core, own_rows, other_rows), either(core, other_rows, own_rows)]
    return (jnp.concatenate(rows, axis=0).astype(BF16),)


def local(
    tokens,
    ln_gain,
    qkv_weight,
    query_pool,
    key_pool,
    value_pool,
    proj_weight,
    skip_weight,
    cotangent,
):
    cot_near = swap(cotangent, "core")

    own_kv, sent_kv, normed, held = fuse(
        front,
        [((32, 256), BF16)] * 2 + [((256, 384), BF16)] * 2,
        "front",
        direct=True,
    )(tokens, ln_gain, qkv_weight, key_pool, value_pool)
    other_kv = swap_z(sent_kv, 2)
    leaving, held = lax.optimization_barrier((cotangent, held))
    cot_far = swap(leaving, "half")
    (copies_kv,) = fuse(copy_pair, [((32, 16, 384), BF16)], "copy_pair")(own_kv, other_kv)
    copies_kv, cot_far, cot_near = lax.optimization_barrier((copies_kv, cot_far, cot_near))
    cot_both = swap(cot_far, "core")
    rows_kv = exchange_pairs(copies_kv)

    mine, theirs, held_cotangent, skipped, d_pooled = fuse(
        middle,
        [
            ((64, 256), BF16),
            ((64, 256), BF16),
            ((64, 768), BF16),
            ((64, 192), F32),
            ((64, 384), BF16),
        ],
        "middle",
    )(
        normed,
        held,
        qkv_weight,
        query_pool,
        cotangent,
        cot_near,
        cot_far,
        cot_both,
        proj_weight,
        skip_weight,
    )
    rows_grad, mixed, returned = fuse(
        attend, [((32, 16, 384), BF16), ((64, 256), F32), ((64, 256), BF16)], "attend"
    )(rows_kv, mine, swap_z(theirs, 1))

    arrived = exchange_pairs(rows_grad)
    own_grad, other_grad = fuse(pair_sum, [((32, 256), BF16)] * 2, "pair_sum")(arrived)
    other_grad = swap_z(other_grad, 2)
    pieces, d_queries, head_part = fuse(
        after, [((18, 96, 128), BF16), ((256, 192), BF16), ((64, 768), BF16)], "after"
    )(mixed, swap_z(returned, 1), normed, query_pool, held_cotangent, proj_weight)

    pieces, d_keys, d_values = weights(
        own_grad, other_grad, normed, key_pool, value_pool, pieces
    )
    arrived = exchange_pairs(pieces)
    kept, sent = fuse(spread, [((192, 384), BF16)] * 2, "spread")(
        d_keys, d_values, d_queries, qkv_weight, d_pooled, head_part, held, ln_gain
    )

    both, sent, staying = fuse(
        mix, [((128, 384), BF16), ((160, 384), BF16), ((64, 192), F32)], "mix"
    )(kept, swap(sent, "core"))
    taken = swap(sent, "half")

    reduced = jnp.sum(arrived.astype(F32), axis=0).astype(BF16)
    reduced, both = lax.optimization_barrier((reduced, both))
    (copies,) = fuse(settle, [((32, 96, 128), BF16)], "settle")(reduced, swap_z(reduced, 2))
    qkv_grad, proj_grad = finish(exchange_pairs(copies))

    own_rows, block_out = fuse(back, [((128, 384), BF16), ((64, 192), BF16)], "back", flops=20 * 10**9)(
        both, taken, staying, skipped
    )
    (input_grad,) = fuse(join, [((256, 384), BF16)], "join")(
        own_rows, swap(own_rows, "core")
    )
    return (block_out, input_grad, qkv_grad, proj_grad)


def solution(mesh):
    grid = Mesh(
        np.asarray(mesh.devices).reshape(4, 4, 4, 2, 2), ("y", "z", "x", "half", "core")
    )
    placed = (
        P(TILE, None),
        P(),
        P(None, HEAD, None),
        P(None, HEAD),
        P(None, HEAD),
        P(None, HEAD),
        P(HEAD, None),
        P(HEAD, None),
        P(TILE, HEAD),
    )
    return jax.shard_map(
        local,
        mesh=grid,
        in_specs=placed,
        out_specs=(P(TILE, HEAD), P(TILE, None), P(None, HEAD, None), P(HEAD, None)),
        check_vma=False,
    )
```
